128 devices in a mesh: grp: 8 (over x_lo, y), tile: 16 (over x_hi, z, core).
Axes of the slice: x: 4 (x_hi: 2, x_lo: 2; x = x_hi * 2 + x_lo), y: 4, z: 4, core: 2. Of those that a mesh axis runs over, the one named last changes fastest.
Arguments:
- pressure: float32 [2, 32, 384, 768], P(None, None, ('grp', 'tile')), may hold values from -6 to 6
- u_wind: float32 [2, 32, 384, 768], P(None, None, ('grp', 'tile')), may hold values from -4 to 4
- v_wind: float32 [2, 32, 384, 768], P(None, None, ('grp', 'tile')), may hold values from -4 to 4
- stiffness: float32 [2, 32, 384, 768], P(None, None, ('grp', 'tile')), may hold values from 0.5 to 2
- vertical: float32 [32, 32], replicated, may hold values from -1 to 1
- nest_row0: int32 [60], replicated, may hold values from 1 to 60, as said below
- nest_col0: int32 [511], replicated, may hold values from 1 to 511, as said below
Outputs:
- pressure_out: float32 [2, 32, 384, 768], P(None, None, ('grp', 'tile'))
- u_out: float32 [2, 32, 384, 768], P(None, None, ('grp', 'tile'))
- v_out: float32 [2, 32, 384, 768], P(None, None, ('grp', 'tile'))
The draws below stay inside these ranges and needn't reach their ends.
Inputs may be any that keep to these rules, and one draw needn't show every extreme that they name: `nest_row0`: each whole number of the range appears exactly once. `nest_col0`: each whole number of the range appears exactly once.
All inputs are finite; a program needn't handle non-finite values.
Results may differ from the reference program's by a relative error of at most 0.0001.
Values sent between devices are 32-bit elements; how exact they have to be, the bound alone decides.
A program may use at most 64 MiB of HBM per device.

```python
import math
import jax
import jax.numpy as jnp
from jax import lax

LEVELS = 32
ROWS_DEV = 3
COLUMNS = 768
RATIO = 3
OUTER = 2
ROWS = 384
WIN_X = 128
WIN_Y = 256


def draw_nest_row0(key, part):
    key = jax.random.fold_in(key, 7)
    count = ROWS // 6 - ROWS_DEV - 1
    return (jax.random.permutation(key, count) + 1).astype(jnp.int32)


def draw_nest_col0(key, part):
    key = jax.random.fold_in(key, 11)
    count = COLUMNS - WIN_Y - 1
    return (jax.random.permutation(key, count) + 1).astype(jnp.int32)


def level_of(rng, dims, split, least, largest):
    def one(axis_at, blocks):
        draws = jax.random.uniform(jax.random.fold_in(jax.random.fold_in(rng, 6), axis_at), (blocks,), jnp.float32, least / len(split), largest / len(split))
        return jnp.repeat(jnp.exp(draws), dims[axis_at] // blocks).reshape((-1,) + (1,) * (len(dims) - axis_at - 1))

    loudness = one(*split[0])
    for cut in split[1:]:
        loudness = loudness * one(*cut)
    return loudness


def bell_draw(stream_key, shape, spread, bound, shards=(), held_as=jnp.bfloat16):
    result = spread * jax.random.normal(stream_key, shape, jnp.float32)
    if shards:
        result = result * level_of(stream_key, shape, shards, -0.22, 0.18)
    return jnp.clip(result, -bound, bound).astype(held_as)


def setup_inputs(seed: int = 0) -> dict:
    seeds = jax.random.split(jax.random.key(seed), 8)
    return {
        "pressure": bell_draw(seeds[0], (2, LEVELS, ROWS, COLUMNS), 1.0, 6.0, ((2, 128),), jnp.float32),
        "u_wind": bell_draw(seeds[1], (2, LEVELS, ROWS, COLUMNS), 0.5, 4.0, ((2, 128),), jnp.float32),
        "v_wind": bell_draw(seeds[2], (2, LEVELS, ROWS, COLUMNS), 0.5, 4.0, ((2, 128),), jnp.float32),
        "stiffness": jnp.clip(jnp.exp(math.log(2.0) - 1.3862944 * jax.random.uniform(seeds[3], (2, LEVELS, ROWS, COLUMNS), jnp.float32) ** level_of(seeds[3], (2, LEVELS, ROWS, COLUMNS), ((2, 128),), -0.2, 0.2)), 0.5, 2.0),
        "vertical": bell_draw(seeds[4], (LEVELS, LEVELS), LEVELS ** -0.5, 1.0, (), jnp.float32),
        "nest_row0": draw_nest_row0(jax.random.fold_in(seeds[7], 71), 0),
        "nest_col0": draw_nest_col0(jax.random.fold_in(seeds[7], 71), 0),
    }


COURANT = 0.3
MIXING = 0.15


def mixlevels(vertical, field):
    return field + MIXING * jnp.einsum("ab,bxy->axy", vertical, field, precision=lax.Precision.HIGHEST)


def velocities(pressure, u_wind, v_wind, above, right_col):
    p_up = jnp.concatenate([pressure[:, 1:], above], axis=1)
    u_new = u_wind - COURANT * (p_up - pressure)
    p_rt = jnp.concatenate([pressure[:, :, 1:], right_col], axis=2)
    v_new = v_wind - COURANT * (p_rt - pressure)
    return u_new, v_new


def pressures(pressure, u_new, v_new, stiffness, vertical, below, left_col):
    u_dn = jnp.concatenate([below, u_new[:, :-1]], axis=1)
    v_dn = jnp.concatenate([left_col, v_new[:, :, :-1]], axis=2)
    q_field = pressure - COURANT * stiffness * ((u_new - u_dn) + (v_new - v_dn))
    return mixlevels(vertical, q_field)


def reference(pressure, u_wind, v_wind, stiffness, vertical, nest_row0, nest_col0):
    row0 = nest_row0[0].astype(jnp.int32)
    col0 = nest_col0[0].astype(jnp.int32)
    zero = jnp.zeros((), jnp.int32)
    par_p, nst_p = pressure[0], pressure[1]
    par_u, nst_u = u_wind[0], u_wind[1]
    par_v, nst_v = v_wind[0], v_wind[1]
    par_k, nst_k = stiffness[0], stiffness[1]
    zrow = jnp.zeros((LEVELS, 1, COLUMNS), jnp.float32)
    for outer in range(OUTER):
        row_p = lax.dynamic_slice(par_p, (zero, row0 + WIN_X, col0), (LEVELS, 1, WIN_Y))
        row_u = lax.dynamic_slice(par_u, (zero, row0 - 1, col0), (LEVELS, 1, WIN_Y))
        col_p = lax.dynamic_slice(par_p, (zero, row0, col0 + WIN_Y), (LEVELS, WIN_X, 1))
        col_v = lax.dynamic_slice(par_v, (zero, row0, col0 - 1), (LEVELS, WIN_X, 1))
        above_n = jnp.repeat(row_p, RATIO, axis=2)
        below_n = jnp.repeat(row_u, RATIO, axis=2)
        right_n = jnp.repeat(col_p, RATIO, axis=1)
        left_n = jnp.repeat(col_v, RATIO, axis=1)
        u_new, v_new = velocities(par_p, par_u, par_v, zrow, par_p[:, :, :1])
        u_new = u_new.at[:, -1].set(0.0)
        par_p = pressures(par_p, u_new, v_new, par_k, vertical, zrow, v_new[:, :, -1:])
        par_u, par_v = u_new, v_new
        for inner in range(RATIO):
            u_new, v_new = velocities(nst_p, nst_u, nst_v, above_n, right_n)
            nst_p = pressures(nst_p, u_new, v_new, nst_k, vertical, below_n, left_n)
            nst_u, nst_v = u_new, v_new
        averaged = nst_p.reshape(LEVELS, WIN_X, RATIO, WIN_Y, RATIO).mean(axis=(2, 4))
        par_p = lax.dynamic_update_slice(par_p, averaged, (zero, row0, col0))
    return (jnp.stack([par_p, nst_p]), jnp.stack([par_u, nst_u]), jnp.stack([par_v, nst_v]))
```

```python
import functools

import jax
import jax.numpy as jnp
from jax import lax
from jax.experimental import pallas as pl
from jax.experimental.pallas import tpu as pltpu
from jax.sharding import PartitionSpec as P

RATIO = 3
OUTER = 2
COURANT = 0.3
MIXING = 0.15
STRIDE = 8
LAST_X0 = 60
MESH = pl.DeviceIdType.MESH
F32 = jnp.float32
BF16 = jnp.bfloat16


def pieces(x):
    a = x.astype(BF16)
    rest = x - a.astype(F32)
    b = rest.astype(BF16)
    c = (rest - b.astype(F32)).astype(BF16)
    return a, b, c


def kernel(
    n, tiles,
    row0_ref, col0_ref, vert_ref, p_in, u_in, v_in, k_in,
    p_out, u_out, v_out,
    n_p, n_u, n_v, n_k, p_p, p_u, p_v, p_k,
    n_ab, n_bl, n_ub, p_ab, p_bl, p_ub,
    g_send, g_mid, a_send, b_send, f_mid, a_row, b_row, fold,
    g_one0, g_one1, g_two0, g_two1, a_recv0, a_recv1, b_recv0, b_recv1, f_one0, f_one1, f_two0, f_two1,
    in_sem, out_sem, nx_send, nx_recv, px_send, px_recv,
    g1_send, g1_recv, g2_send, g2_recv, e_send, e_recv,
    f1_send, f1_recv, f2_send, f2_recv,
):
    levels, cols = n_k.shape[1], n_k.shape[2]
    win = cols // RATIO
    me = lax.axis_index("grp") * tiles + lax.axis_index("tile")
    first, last = me == 0, me == n - 1
    x0, y0 = row0_ref[0], col0_ref[0]
    shift_b, shift_c = lax.shift_right_logical(x0, 3), x0 & (STRIDE - 1)
    own = RATIO * me
    owners = (LAST_X0 + n) // RATIO + 1
    a_low = (1 + n) // RATIO
    a_count = owners - a_low
    b_count = (LAST_X0 - 1) // RATIO + 1
    finish = []
    g_one, g_two, a_recv, b_recv = (g_one0, g_one1), (g_two0, g_two1), (a_recv0, a_recv1), (b_recv0, b_recv1)
    f_one, f_two = (f_one0, f_one1), (f_two0, f_two1)

    def dev(d):
        return (d // tiles, d % tiles)

    def send(src, dst, s_sem, r_sem, to, cond=None, wait=True):
        copy = pltpu.make_async_remote_copy(
            src_ref=src, dst_ref=dst, send_sem=s_sem, recv_sem=r_sem, device_id=dev(to), device_id_type=MESH
        )
        if cond is None:
            copy.start()
            if wait:
                finish.append(copy.wait_send)
        else:
            pl.when(cond)(copy.start)
            if wait:
                finish.append(lambda: pl.when(cond)(copy.wait_send))

    def arrived(ref, sem, cond=None):
        def go():
            pltpu.make_async_copy(ref, ref, sem).wait()
        if cond is None:
            go()
        else:
            pl.when(cond)(go)

    loads = {}
    for at, (name, src, g, dst) in enumerate((
        ("pp", p_in, 0, p_p.at[0]), ("pv", v_in, 0, p_v), ("pu", u_in, 0, p_u),
        ("np", p_in, 1, n_p.at[0]), ("nu", u_in, 1, n_u), ("nv", v_in, 1, n_v),
        ("nk", k_in, 1, n_k), ("pk", k_in, 0, p_k),
    )):
        loads[name] = pltpu.make_async_copy(src.at[g], dst, in_sem.at[at])
        loads[name].start()

    def exchange(src, s, ab, bl, ss, rs):
        send(src.at[2], bl.at[s], ss.at[2 * s], rs.at[2 * s], me + 1, ~last)
        send(src.at[0], ab.at[s], ss.at[2 * s + 1], rs.at[2 * s + 1], me - 1, ~first)

    exchange(p_in.at[1], 0, n_ab, n_bl, nx_send, nx_recv)
    send(u_in.at[1, 2], n_ub, nx_send.at[12], nx_recv.at[12], me + 1, ~last)

    lane = lax.broadcasted_iota(jnp.int32, (levels, cols), 1)
    lane128 = lax.broadcasted_iota(jnp.int32, (levels, 128), 1)
    level128 = lax.broadcasted_iota(jnp.int32, (levels, 128), 0)

    def valid_edges():
        for w in range(2):
            base = me + n * w
            for m in range(4):
                owner = base // RATIO + m
                slot = base % RATIO + 7 - RATIO * m
                cond = (slot >= 0) & (owner < owners)
                if w == 1:
                    cond = cond & (me < 8 * STRIDE)
                yield owner, cond, slot, 4 * w + m

    def start_ghosts(o, pp):
        gsum = jnp.zeros((8, 128), F32)
        row8 = lax.broadcasted_iota(jnp.int32, (8, 128), 0)
        for j in range(RATIO):
            right = jnp.sum(jnp.where(lane == y0 + win, pp[j], 0.0), axis=1, keepdims=True)
            left = jnp.sum(jnp.where(lane == y0 - 1, p_v[j], 0.0), axis=1, keepdims=True)
            both = jnp.where(level128 == lane128, right, 0.0) + jnp.where(level128 == lane128 - levels, left, 0.0)
            gsum = jnp.where(row8 == j, jnp.sum(both, axis=0, keepdims=True), gsum)
        g_send[o] = gsum
        for k in range(10):
            base = own + k - 7
            m = -((k - 7) // RATIO)
            slot = 4 * (base // n) + m
            to = base % n
            cond = (base >= 0) & (me < owners)
            pick = g_one[o].at[jnp.clip(slot, 0, 7)]

            @pl.when(cond & (to == me))
            def _():
                g_one[o][jnp.clip(slot, 0, 7)] = g_send[o]
            send(g_send.at[o], pick, g1_send.at[o, k], g1_recv.at[o, jnp.clip(slot, 0, 7)], to, cond & (to != me))

        def pick_row(field, target):
            out = jnp.zeros((levels, cols), F32)
            for j in range(RATIO):
                out = jnp.where(target == own + j, field[j], out)
            return pltpu.roll(out, cols - y0, axis=1)[:, :win]

        is_a = (me >= a_low) & (me < owners)
        is_b = me < b_count

        @pl.when(is_a)
        def _():
            a_send[o] = pick_row(pp, x0 + n)
        send(a_send.at[o], a_recv[o].at[jnp.clip(me - a_low, 0, a_count - 1)], e_send.at[o, 0], e_recv.at[o, 0], n - 1, is_a)

        @pl.when(is_b)
        def _():
            b_send[o] = pick_row(p_u, x0 - 1)

        @pl.when(first)
        def _():
            b_recv[o][0] = b_send[o]
        send(b_send.at[o], b_recv[o].at[jnp.clip(me, 0, b_count - 1)], e_send.at[o, 1], e_recv.at[o, 1], 0, is_b & ~first)

    def pass_ghosts(o):
        for owner, cond, _, here in valid_edges():
            arrived(g_one[o].at[here], g1_recv.at[o, here], cond & (owner != me))
        wrapped = me < STRIDE * shift_b
        rem = jnp.where(wrapped, (me + n) % RATIO, me % RATIO) + shift_c
        slot = jnp.where(wrapped, 4, 0) + rem // RATIO
        row8 = lax.broadcasted_iota(jnp.int32, (8, 128), 0)
        block = g_one[o][slot]
        row = jnp.sum(jnp.where(row8 == rem % RATIO, block, 0.0), axis=0, keepdims=True)
        g_mid[o] = jnp.broadcast_to(row, (8, 128))
        g_two[o][0] = jnp.broadcast_to(row, (8, 128))
        for b in range(1, 8):
            send(g_mid.at[o], g_two[o].at[b], g2_send.at[o], g2_recv.at[o], (me + n - STRIDE * b) % n, wait=False)
        finish.append(lambda: arrived(g_two[o].at[pl.ds(1, 7)], g2_send.at[o]))

    def take_ghosts(o):
        arrived(g_two[o].at[pl.ds(1, 7)], g2_recv.at[o])
        row = g_two[o][shift_b][0:1]
        right = jnp.sum(jnp.where(level128 == lane128, row, 0.0), axis=1, keepdims=True)
        left = jnp.sum(jnp.where(level128 == lane128 - levels, row, 0.0), axis=1, keepdims=True)

        def widen(x):
            a, b, c = pieces(x)
            stack = jnp.concatenate([a, b, c], axis=0)
            wide = lax.dot_general(stack, fold[...], (((1,), (1,)), ((), ())), preferred_element_type=F32)
            return (wide[:levels] + wide[levels:2 * levels]) + wide[2 * levels:]

        @pl.when(last)
        def _():
            arrived(a_recv[o], e_recv.at[o, 0])
            a_row[...] = widen(a_recv[o][jnp.clip((x0 + n) // RATIO - a_low, 0, a_count - 1)])

        @pl.when(first)
        def _():
            arrived(b_recv[o].at[pl.ds(1, b_count - 1)], e_recv.at[o, 1])
            b_row[...] = widen(b_recv[o][jnp.clip((x0 - 1) // RATIO, 0, b_count - 1)])
            n_ub[...] = b_row[...]

        return jnp.broadcast_to(right, (levels, 128)), jnp.broadcast_to(left, (levels, 128))

    def from_right(x, edge):
        moved = pltpu.roll(x, cols - 1, axis=1)
        if edge is None:
            return moved
        tail = jnp.where(lane128 == 127, edge, moved[:, cols - 128:])
        return jnp.concatenate([moved[:, :cols - 128], tail], axis=1)

    def from_left(x, edge):
        moved = pltpu.roll(x, 1, axis=1)
        if edge is None:
            return moved
        head = jnp.where(lane128 == 0, edge, moved[:, :128])
        return jnp.concatenate([head, moved[:, 128:]], axis=1)

    def mixed(q, mix):
        a, b, c = pieces(q)
        return q + jnp.dot(mix, jnp.concatenate([a, b, a, b, c, a], axis=0), preferred_element_type=F32)

    def new_pressure(p, k, u, below, v, left, mix):
        return mixed(p - COURANT * k * ((u - below) + (v - from_left(v, left))), mix)

    def nest_substep(s, right, left, mix):
        p, new = n_p.at[s], n_p.at[s + 1]
        for r in range(RATIO):
            n_v[r] = n_v[r] - COURANT * (from_right(p[r], right) - p[r])
        for r in range(2):
            n_u[r] = n_u[r] - COURANT * (p[r + 1] - p[r])
        arrived(n_bl.at[s], nx_recv.at[2 * s], ~first)
        if s == 0:
            arrived(n_ub, nx_recv.at[12], ~first)

        @pl.when(~first)
        def _():
            n_ub[...] = n_ub[...] - COURANT * (p[0] - n_bl[s])
        new[0] = new_pressure(p[0], n_k[0], n_u[0], n_ub[...], n_v[0], left, mix)
        if s < 5:
            send(new.at[0], n_ab.at[s + 1], nx_send.at[2 * s + 3], nx_recv.at[2 * s + 3], me - 1, ~first)

        arrived(n_ab.at[s], nx_recv.at[2 * s + 1], ~last)

        @pl.when(last)
        def _():
            n_ab[s] = a_row[...]
        n_u[2] = n_u[2] - COURANT * (n_ab[s] - p[2])
        new[2] = new_pressure(p[2], n_k[2], n_u[2], n_u[1], n_v[2], left, mix)
        if s < 5:
            send(new.at[2], n_bl.at[s + 1], nx_send.at[2 * s + 2], nx_recv.at[2 * s + 2], me + 1, ~last)
        new[1] = new_pressure(p[1], n_k[1], n_u[1], n_u[0], n_v[1], left, mix)

    def parent_substep(s, mix):
        p, new = p_p.at[s], p_p.at[s + 1]
        arrived(p_bl.at[s], px_recv.at[2 * s], ~first)
        arrived(p_ab.at[s], px_recv.at[2 * s + 1], ~last)
        if s == 0:
            arrived(p_ub, px_recv.at[4], ~first)
        for r in range(RATIO):
            p_v[r] = p_v[r] - COURANT * (from_right(p[r], None) - p[r])
        for r in range(2):
            p_u[r] = p_u[r] - COURANT * (p[r + 1] - p[r])
        p_u[2] = jnp.where(last, 0.0, p_u[2] - COURANT * (p_ab[s] - p[2]))
        p_ub[...] = jnp.where(first, 0.0, p_ub[...] - COURANT * (p[0] - p_bl[s]))
        for r in range(RATIO):
            below = p_ub[...] if r == 0 else p_u[r - 1]
            new[r] = new_pressure(p[r], p_k[r], p_u[r], below, p_v[r], None, mix)

    def start_feedback(o):
        rows = n_p.at[3 * (o + 1)]
        a, b, c = pieces((rows[0] + rows[1]) + rows[2])
        stack = jnp.concatenate([a, b, c], axis=0)
        mean = jnp.dot(stack, fold[...], preferred_element_type=F32)
        mean = ((mean[:levels] + mean[levels:2 * levels]) + mean[2 * levels:]) * (1.0 / (RATIO * RATIO))
        f_one[o][0] = mean
        for b in range(1, 8):
            send(f_one[o].at[0], f_one[o].at[b], f1_send.at[o], f1_recv.at[o], (me + STRIDE * b) % n, wait=False)
        finish.append(lambda: arrived(f_one[o].at[pl.ds(1, 7)], f1_send.at[o]))

    def pass_feedback(o):
        arrived(f_one[o].at[pl.ds(1, 7)], f1_recv.at[o])
        f_mid[o] = f_one[o][shift_b]
        for owner, cond, slot, here in valid_edges():
            slot = jnp.clip(slot, 0, 9)

            @pl.when(cond & (owner == me))
            def _():
                f_two[o][slot] = f_mid[o]
            send(f_mid.at[o], f_two[o].at[slot], f2_send.at[o, here], f2_recv.at[o, slot], owner % n, cond & (owner != me))

    def take_feedback(o, pp):
        for k in range(10):
            base = own + k - 7
            arrived(f_two[o].at[k], f2_recv.at[o, k], (base >= 0) & (me < owners) & (base % n != me))
        under = (lane >= y0) & (lane < y0 + win)
        for j in range(RATIO):
            row = own + j
            value = f_two[o][j - shift_c + 7]
            value = pltpu.roll(jnp.concatenate([value, jnp.zeros((levels, cols - win), F32)], axis=1), y0, axis=1)
            inside = ((row >= x0) & (row < x0 + n)).astype(jnp.int32)
            pp[j] = jnp.where(under & (jnp.broadcast_to(inside, (levels, cols)) > 0), value, pp[j])

    exchange(p_in.at[0], 0, p_ab, p_bl, px_send, px_recv)
    send(u_in.at[0, 2], p_ub, px_send.at[4], px_recv.at[4], me + 1, ~last)
    for name in ("pp", "pv", "pu"):
        loads[name].wait()
    start_ghosts(0, p_p.at[0])

    spot = lax.broadcasted_iota(jnp.int32, (cols, win), 0) - RATIO * lax.broadcasted_iota(jnp.int32, (cols, win), 1)
    fold[...] = jnp.where((spot >= 0) & (spot < RATIO), 1.0, 0.0).astype(BF16)
    block = lax.broadcasted_iota(jnp.int32, (levels, 6 * levels), 1)
    copies = (block % levels == lax.broadcasted_iota(jnp.int32, (levels, 6 * levels), 0)).astype(F32)
    wide = jnp.dot(MIXING * vert_ref[...], copies, precision=lax.Precision.HIGHEST, preferred_element_type=F32)
    m1, m2, m3 = (x.astype(F32) for x in pieces(wide))
    part = block // levels
    mix = jnp.where(part >= 5, m3, jnp.where((part == 2) | (part == 3), m2, m1)).astype(BF16)

    pass_ghosts(0)
    for name in ("np", "nu", "nv", "nk", "pk"):
        loads[name].wait()
    right, left = take_ghosts(0)
    nest_substep(0, right, left, mix)
    parent_substep(0, mix)
    start_ghosts(1, p_p.at[1])
    nest_substep(1, right, left, mix)
    pass_ghosts(1)
    nest_substep(2, right, left, mix)
    start_feedback(0)
    right, left = take_ghosts(1)
    nest_substep(3, right, left, mix)
    pass_feedback(0)
    nest_substep(4, right, left, mix)
    take_feedback(0, p_p.at[1])
    exchange(p_p.at[1], 1, p_ab, p_bl, px_send, px_recv)
    nest_substep(5, right, left, mix)
    start_feedback(1)
    outs = []

    def store(src, dst):
        outs.append(pltpu.make_async_copy(src, dst, out_sem.at[len(outs)]))
        outs[-1].start()
    store(n_p.at[6], p_out.at[1])
    store(n_u, u_out.at[1])
    store(n_v, v_out.at[1])
    parent_substep(1, mix)
    store(p_u, u_out.at[0])
    store(p_v, v_out.at[0])
    pass_feedback(1)
    take_feedback(1, p_p.at[2])
    store(p_p.at[2], p_out.at[0])
    for wait in finish:
        wait()
    for copy in outs:
        copy.wait()


def per_device(n, tiles, pressure, u_wind, v_wind, stiffness, vertical, nest_row0, nest_col0):
    fields = [jnp.transpose(x, (0, 2, 1, 3)) for x in (pressure, u_wind, v_wind, stiffness)]
    _, rows, levels, cols = fields[0].shape
    win = cols // RATIO
    slab = (rows, levels, cols)
    row = (levels, cols)
    owners = (LAST_X0 + n) // RATIO + 1
    a_count = owners - (1 + n) // RATIO
    b_count = (LAST_X0 - 1) // RATIO + 1
    vmem = lambda *shape: pltpu.VMEM(shape, F32)
    dma = lambda *shape: pltpu.SemaphoreType.DMA(shape)
    outs = pl.pallas_call(
        functools.partial(kernel, n, tiles),
        out_shape=[jax.ShapeDtypeStruct((2,) + slab, F32)] * 3,
        in_specs=[pl.BlockSpec(memory_space=pltpu.SMEM)] * 2
        + [pl.BlockSpec(memory_space=pltpu.VMEM)]
        + [pl.BlockSpec(memory_space=pl.ANY)] * 4,
        out_specs=[pl.BlockSpec(memory_space=pl.ANY)] * 3,
        scratch_shapes=[
            vmem(7, *slab), vmem(*slab), vmem(*slab), vmem(*slab),
            vmem(3, *slab), vmem(*slab), vmem(*slab), vmem(*slab),
            vmem(6, *row), vmem(6, *row), vmem(*row), vmem(2, *row), vmem(2, *row), vmem(*row),
            vmem(OUTER, 8, 128), vmem(OUTER, 8, 128), vmem(OUTER, levels, win), vmem(OUTER, levels, win),
            vmem(OUTER, levels, win), vmem(*row), vmem(*row), pltpu.VMEM((cols, win), BF16),
            *[vmem(8, 8, 128)] * 4,
            *[vmem(a_count, levels, win)] * 2, *[vmem(b_count, levels, win)] * 2,
            *[vmem(8, levels, win)] * 2, *[vmem(10, levels, win)] * 2,
            dma(8), dma(6), dma(13), dma(13), dma(5), dma(5),
            dma(OUTER, 10), dma(OUTER, 8), dma(OUTER), dma(OUTER), dma(OUTER, 2), dma(OUTER, 2),
            dma(OUTER), dma(OUTER), dma(OUTER, 8), dma(OUTER, 10),
        ],
        compiler_params=pltpu.CompilerParams(has_side_effects=True, vmem_limit_bytes=48 * 1024 * 1024),
        cost_estimate=pl.CostEstimate(flops=300_000_000, bytes_accessed=4_200_000, transcendentals=0),
    )(nest_row0, nest_col0, vertical, *fields)
    return tuple(jnp.transpose(x, (0, 2, 1, 3)) for x in outs)


def solution(mesh):
    spec = P(None, None, ("grp", "tile"), None)
    tiles = mesh.shape["tile"]
    return jax.shard_map(
        functools.partial(per_device, mesh.shape["grp"] * tiles, tiles),
        mesh=mesh,
        in_specs=(spec, spec, spec, spec, P(), P(), P()),
        out_specs=(spec, spec, spec),
        check_vma=False,
    )
```

```python
import functools

import jax
import jax.numpy as jnp
from jax import lax
from jax.experimental import pallas as pl
from jax.experimental.pallas import tpu as pltpu
from jax.sharding import PartitionSpec as P

RATIO = 3
OUTER = 2
COURANT = 0.3
MIXING = 0.15
STRIDE = 8
LAST_X0 = 60
MESH = pl.DeviceIdType.MESH
F32 = jnp.float32
BF16 = jnp.bfloat16


def pieces(x):
    a = x.astype(BF16)
    rest = x - a.astype(F32)
    b = rest.astype(BF16)
    c = (rest - b.astype(F32)).astype(BF16)
    return a, b, c


def kernel(
    n, tiles,
    row0_ref, col0_ref, vert_ref, p_in, u_in, v_in, k_in,
    p_out, u_out, v_out,
    n_p, n_u, n_v, n_k, p_p, p_u, p_v, p_k,
    g_send, g_mid, a_send, b_send, f_mid, a_row, b_row, edge, fold, mix,
    g_one0, g_one1, g_two0, g_two1, a_recv0, a_recv1, b_recv0, b_recv1, f_one0, f_one1, f_two0, f_two1,
    in_sem, out_sem, ni_send, ni_recv, nx_send, nx_recv, nm_send, nm_recv, px_send, px_recv,
    g1_send, g1_recv, g2_send, g2_recv, e_send, e_recv,
    f1_send, f1_recv, f2_send, f2_recv,
):
    levels, cols = n_k.shape[1], n_k.shape[2]
    win = cols // RATIO
    me = lax.axis_index("grp") * tiles + lax.axis_index("tile")
    first, last = me == 0, me == n - 1
    x0, y0 = row0_ref[0], col0_ref[0]
    shift_b, shift_c = lax.shift_right_logical(x0, 3), x0 & (STRIDE - 1)
    own = RATIO * me
    owners = (LAST_X0 + n) // RATIO + 1
    a_low = (1 + n) // RATIO
    a_count = owners - a_low
    b_count = (LAST_X0 - 1) // RATIO + 1
    finish = []
    g_one, g_two, a_recv, b_recv = (g_one0, g_one1), (g_two0, g_two1), (a_recv0, a_recv1), (b_recv0, b_recv1)
    f_one, f_two = (f_one0, f_one1), (f_two0, f_two1)

    def dev(d):
        return (d // tiles, d % tiles)

    def remote(src, dst, s_sem, r_sem, to):
        return pltpu.make_async_remote_copy(
            src_ref=src, dst_ref=dst, send_sem=s_sem, recv_sem=r_sem, device_id=dev(to), device_id_type=MESH
        )

    def send(src, dst, s_sem, r_sem, to, cond):
        copy = remote(src, dst, s_sem, r_sem, to)
        pl.when(cond)(copy.start)
        finish.append(lambda: pl.when(cond)(copy.wait_send))

    def loop(low, high, body):
        lax.fori_loop(low, high, lambda i, _: (body(i), 0)[1], 0)

    def send_each(count, make):
        def start(i):
            copy, cond = make(i)
            pl.when(cond)(copy.start)

        def end(i):
            copy, cond = make(i)
            pl.when(cond)(copy.wait_send)
        loop(0, count, start)
        finish.append(lambda: loop(0, count, end))

    def arrived(ref, sem, cond=True):
        @pl.when(cond)
        def _():
            pltpu.make_async_copy(ref, ref, sem).wait()

    loads = {}
    for at, (name, src, g, dst) in enumerate((
        ("pp", p_in, 0, p_p.at[0, pl.ds(1, 3)]), ("pv", v_in, 0, p_v), ("pu", u_in, 0, p_u.at[pl.ds(1, 3)]),
        ("np", p_in, 1, n_p.at[0, pl.ds(2, 3)]), ("nu", u_in, 1, n_u.at[pl.ds(2, 3)]),
        ("nv", v_in, 1, n_v.at[pl.ds(1, 3)]), ("nk", k_in, 1, n_k.at[pl.ds(1, 3)]), ("pk", k_in, 0, p_k),
    )):
        loads[name] = pltpu.make_async_copy(src.at[g], dst, in_sem.at[at])
        loads[name].start()

    def parent_exchange(s, rows):
        send(rows.at[2], p_p.at[s, 0], px_send.at[s, 0], px_recv.at[s, 0], me + 1, ~last)
        send(rows.at[0], p_p.at[s, 4], px_send.at[s, 1], px_recv.at[s, 1], me - 1, ~first)

    parent_exchange(0, p_in.at[0])
    send(u_in.at[0, 2], p_u.at[0], px_send.at[0, 2], px_recv.at[0, 2], me + 1, ~last)
    to_up = (
        (p_in.at[1, pl.ds(1, 2)], n_p.at[0, pl.ds(0, 2)]), (u_in.at[1, pl.ds(1, 2)], n_u.at[pl.ds(0, 2)]),
        (v_in.at[1, 2], n_v.at[0]), (k_in.at[1, 2], n_k.at[0]),
    )
    to_down = (
        (p_in.at[1, pl.ds(0, 2)], n_p.at[0, pl.ds(5, 2)]), (u_in.at[1, 0], n_u.at[5]),
        (v_in.at[1, 0], n_v.at[4]), (k_in.at[1, 0], n_k.at[4]),
    )
    for i in range(4):
        send(*to_up[i], ni_send.at[0, i], ni_recv.at[0, i], me + 1, ~last)
        send(*to_down[i], ni_send.at[1, i], ni_recv.at[1, i], me - 1, ~first)

    lane = lax.broadcasted_iota(jnp.int32, (levels, cols), 1)
    lane128 = lax.broadcasted_iota(jnp.int32, (levels, 128), 1)
    level128 = lax.broadcasted_iota(jnp.int32, (levels, 128), 0)
    row8 = lax.broadcasted_iota(jnp.int32, (8, 128), 0)

    def start_ghosts(o, pp, pu):
        def gather(j, total):
            right = jnp.sum(jnp.where(lane == y0 + win, pp[j], 0.0), axis=1, keepdims=True)
            left = jnp.sum(jnp.where(lane == y0 - 1, p_v[j], 0.0), axis=1, keepdims=True)
            both = jnp.where(level128 == lane128, right, 0.0) + jnp.where(level128 == lane128 - levels, left, 0.0)
            return jnp.where(row8 == j, jnp.sum(both, axis=0, keepdims=True), total)
        g_send[o] = lax.fori_loop(0, RATIO, gather, jnp.zeros((8, 128), F32))

        def column(k):
            base = own + k - STRIDE
            slot = jnp.where(base >= n, 4, 0) + 3 - k // RATIO
            to = (base + n) % n
            cond = (base >= 0) & (me < owners)

            @pl.when(cond & (to == me))
            def _():
                g_one[o][slot] = g_send[o]
            copy = remote(g_send.at[o], g_one[o].at[slot], g1_send.at[o, k], g1_recv.at[o, slot], to)
            return copy, cond & (to != me)
        send_each(STRIDE + 4, column)

        def pick_row(field, target):
            out = jnp.zeros((levels, cols), F32)
            for j in range(RATIO):
                out = jnp.where(target == own + j, field[j], out)
            return pltpu.roll(out, cols - y0, axis=1)[:, :win]

        is_a = (me >= a_low) & (me < owners)
        is_b = me < b_count

        @pl.when(is_a)
        def _():
            a_send[o] = pick_row(pp, x0 + n)
        send(a_send.at[o], a_recv[o].at[jnp.clip(me - a_low, 0, a_count - 1)], e_send.at[o, 0], e_recv.at[o, 0], n - 1, is_a)

        @pl.when(is_b)
        def _():
            b_send[o] = pick_row(pu, x0 - 1)

        @pl.when(first)
        def _():
            b_recv[o][0] = b_send[o]
        send(b_send.at[o], b_recv[o].at[jnp.clip(me, 0, b_count - 1)], e_send.at[o, 1], e_recv.at[o, 1], 0, is_b & ~first)

    def pass_ghosts(o):
        for w in range(2):
            base = me + n * w
            for m in range(4):
                owner = (base + 2) // RATIO - 1 + m
                cond = (owner >= 0) & (owner < owners) & (owner != me)
                if w == 1:
                    cond = cond & (me < 8 * STRIDE)
                arrived(g_one[o].at[4 * w + m], g1_recv.at[o, 4 * w + m], cond)
        wrapped = me < STRIDE * shift_b
        rem = jnp.where(wrapped, (me + n + 2) % RATIO, (me + 2) % RATIO) + shift_c
        rows = jnp.zeros((8, 128), F32)
        for t in range(3):
            block = g_one[o][jnp.where(wrapped, 4, 0) + (rem + t) // RATIO]
            row = jnp.sum(jnp.where(row8 == (rem + t) % RATIO, block, 0.0), axis=0, keepdims=True)
            rows = jnp.where(row8 == t, row, rows)
        g_mid[o] = rows
        g_two[o][0] = rows

        def onward(i):
            b = i + 1
            return remote(g_mid.at[o], g_two[o].at[b], g2_send.at[o, i], g2_recv.at[o], (me + n - STRIDE * b) % n), True
        send_each(7, onward)

    def take_ghosts(o):
        arrived(g_two[o].at[pl.ds(1, 7)], g2_recv.at[o])
        rows = g_two[o][shift_b]
        for t in range(3):
            row = rows[t:t + 1]
            right = jnp.sum(jnp.where(level128 == lane128, row, 0.0), axis=1, keepdims=True)
            left = jnp.sum(jnp.where(level128 == lane128 - levels, row, 0.0), axis=1, keepdims=True)
            edge[t, 0] = jnp.broadcast_to(right, (levels, 128))
            edge[t, 1] = jnp.broadcast_to(left, (levels, 128))

        def widen(x):
            a, b, c = pieces(x)
            stack = jnp.concatenate([a, b, c], axis=0)
            wide = lax.dot_general(stack, fold[...], (((1,), (1,)), ((), ())), preferred_element_type=F32)
            return (wide[:levels] + wide[levels:2 * levels]) + wide[2 * levels:]

        @pl.when(last)
        def _():
            arrived(a_recv[o], e_recv.at[o, 0])
            a_row[...] = widen(a_recv[o][jnp.clip((x0 + n) // RATIO - a_low, 0, a_count - 1)])

        @pl.when(first)
        def _():
            arrived(b_recv[o].at[pl.ds(1, b_count - 1)], e_recv.at[o, 1])
            b_row[...] = widen(b_recv[o][jnp.clip((x0 - 1) // RATIO, 0, b_count - 1)])

    def from_right(x, ghost):
        moved = pltpu.roll(x, cols - 1, axis=1)
        if ghost is None:
            return moved
        tail = jnp.where(lane128 == 127, ghost, moved[:, cols - 128:])
        return jnp.concatenate([moved[:, :cols - 128], tail], axis=1)

    def from_left(x, ghost):
        moved = pltpu.roll(x, 1, axis=1)
        if ghost is None:
            return moved
        head = jnp.where(lane128 == 0, ghost, moved[:, :128])
        return jnp.concatenate([head, moved[:, 128:]], axis=1)

    def new_pressure(p, k, u, below, v, left):
        q = p - COURANT * k * ((u - below) + (v - from_left(v, left)))
        a, b, c = pieces(q)
        return q + jnp.dot(mix[...], jnp.concatenate([a, b, a, b, c, a], axis=0), preferred_element_type=F32)

    def nest_u(s, i):
        n_u[i] = n_u[i] - COURANT * (n_p[s, i + 1] - n_p[s, i])

    def nest_v(s, i, t):
        p = n_p[s, i + 1]
        v = n_v[i] - COURANT * (from_right(p, edge[t, 0]) - p)
        n_v[i] = v
        return p, v

    def nest_row(s, i, t):
        nest_u(s, i + 1)

        @pl.when(first & (i == 0))
        def _():
            n_u[1] = b_row[...]
        p, v = nest_v(s, i, t)
        n_p[s + 1, i + 1] = new_pressure(p, n_k[i], n_u[i + 1], n_u[i], v, edge[t, 1])

    def above_nest(s):
        @pl.when(last)
        def _():
            n_p[s, 5] = a_row[...]

    def nest_first(s):
        above_nest(s)
        nest_u(s, 0)
        loop(0, 5, lambda i: nest_row(s, i, (i + 2) // RATIO))
        if s < 4:
            send(n_p.at[s + 1, 3], n_p.at[s + 1, 0], nm_send.at[s // 2, 0], nm_recv.at[s // 2, 0], me + 1, ~last)
            send(n_p.at[s + 1, 3], n_p.at[s + 1, 6], nm_send.at[s // 2, 1], nm_recv.at[s // 2, 1], me - 1, ~first)

    def nest_second(s):
        above_nest(s)
        nest_u(s, 1)

        @pl.when(first)
        def _():
            n_u[1] = b_row[...]

        def up(i):
            return remote(n_p.at[s + 1, i + 3], n_p.at[s + 1, i], nx_send.at[s // 2, 0, i], nx_recv.at[s // 2, 0, i], me + 1)

        def down(i):
            return remote(n_p.at[s + 1, i + 2], n_p.at[s + 1, i + 5], nx_send.at[s // 2, 1, i], nx_recv.at[s // 2, 1, i], me - 1)

        def row(r):
            nest_row(s, r + 1, 1)
            if s < 5:
                pl.when((r >= 1) & ~last)(lambda: up(jnp.maximum(r - 1, 0)).start())
                pl.when((r <= 1) & ~first)(lambda: down(jnp.minimum(r, 1)).start())
        loop(0, 3, row)
        if s < 5:
            for i in range(2):
                finish.append(lambda i=i: pl.when(~last)(up(i).wait_send))
                finish.append(lambda i=i: pl.when(~first)(down(i).wait_send))
            nest_v(s, 0, 0)
            nest_v(s, 4, 2)
            arrived(n_p.at[s, 0], nm_recv.at[s // 2, 0], ~first)
            arrived(n_p.at[s, 6], nm_recv.at[s // 2, 1], ~last)
            nest_u(s, 0)
            nest_u(s, 5)

    def nest_arrived(s):
        for i in range(2):
            arrived(n_p.at[s, i], nx_recv.at[s // 2 - 1, 0, i], ~first)
            arrived(n_p.at[s, 5 + i], nx_recv.at[s // 2 - 1, 1, i], ~last)

    def parent_substep(s):
        arrived(p_p.at[s, 0], px_recv.at[s, 0], ~first)
        arrived(p_p.at[s, 4], px_recv.at[s, 1], ~last)
        if s == 0:
            arrived(p_u.at[0], px_recv.at[0, 2], ~first)

        def parent_u(i):
            p_u[i] = p_u[i] - COURANT * (p_p[s, i + 1] - p_p[s, i])

            @pl.when((first & (i == 0)) | (last & (i == RATIO)))
            def _():
                p_u[i] = jnp.zeros((levels, cols), F32)
        parent_u(0)

        def row(r):
            parent_u(r + 1)
            p = p_p[s, r + 1]
            v = p_v[r] - COURANT * (from_right(p, None) - p)
            p_v[r] = v
            p_p[s + 1, r + 1] = new_pressure(p, p_k[r], p_u[r + 1], p_u[r], v, None)
        loop(0, RATIO, row)

    def owner_edges():
        for w in range(2):
            base = me + n * w
            for m in range(4):
                owner = base // RATIO + m
                slot = base % RATIO + 7 - RATIO * m
                cond = (slot >= 0) & (owner < owners)
                if w == 1:
                    cond = cond & (me < 8 * STRIDE)
                yield owner, cond, jnp.clip(slot, 0, 9), 4 * w + m

    def start_feedback(o):
        rows = n_p.at[3 * (o + 1)]
        a, b, c = pieces((rows[2] + rows[3]) + rows[4])
        mean = jnp.dot(jnp.concatenate([a, b, c], axis=0), fold[...], preferred_element_type=F32)
        f_one[o][0] = ((mean[:levels] + mean[levels:2 * levels]) + mean[2 * levels:]) * (1.0 / (RATIO * RATIO))

        def onward(i):
            b = i + 1
            return remote(f_one[o].at[0], f_one[o].at[b], f1_send.at[o, i], f1_recv.at[o], (me + STRIDE * b) % n), True
        send_each(7, onward)

    def pass_feedback(o):
        arrived(f_one[o].at[pl.ds(1, 7)], f1_recv.at[o])
        f_mid[o] = f_one[o][shift_b]
        for owner, cond, slot, here in owner_edges():
            @pl.when(cond & (owner == me))
            def _():
                f_two[o][slot] = f_mid[o]
            send(f_mid.at[o], f_two[o].at[slot], f2_send.at[o, here], f2_recv.at[o, slot], owner % n, cond & (owner != me))

    def take_feedback(o, source, target):
        def wait(k):
            base = own + k - 7
            arrived(f_two[o].at[k], f2_recv.at[o, k], (base >= 0) & (me < owners) & ((base + n) % n != me))
        loop(0, 10, wait)
        under = (lane >= y0) & (lane < y0 + win)

        def place(j):
            row = own + j
            value = f_two[o][j - shift_c + 7]
            value = pltpu.roll(jnp.concatenate([value, jnp.zeros((levels, cols - win), F32)], axis=1), y0, axis=1)
            inside = ((row >= x0) & (row < x0 + n)).astype(jnp.int32)
            target[j] = jnp.where(under & (jnp.broadcast_to(inside, (levels, cols)) > 0), value, source[j])
        loop(0, RATIO, place)

    for name in ("pp", "pv", "pu"):
        loads[name].wait()
    parent_rows = [p_p.at[s, pl.ds(1, 3)] for s in range(3)]
    start_ghosts(0, parent_rows[0], p_u.at[pl.ds(1, 3)])

    spot = lax.broadcasted_iota(jnp.int32, (cols, win), 0) - RATIO * lax.broadcasted_iota(jnp.int32, (cols, win), 1)
    fold[...] = jnp.where((spot >= 0) & (spot < RATIO), 1.0, 0.0).astype(BF16)
    block = lax.broadcasted_iota(jnp.int32, (levels, 6 * levels), 1)
    copies = (block % levels == lax.broadcasted_iota(jnp.int32, (levels, 6 * levels), 0)).astype(F32)
    wide = jnp.dot(MIXING * vert_ref[...], copies, precision=lax.Precision.HIGHEST, preferred_element_type=F32)
    m1, m2, m3 = (x.astype(F32) for x in pieces(wide))
    part = block // levels
    mix[...] = jnp.where(part >= 5, m3, jnp.where((part == 2) | (part == 3), m2, m1)).astype(BF16)

    loads["pk"].wait()
    pass_ghosts(0)
    parent_substep(0)
    start_ghosts(1, parent_rows[1], p_u.at[pl.ds(1, 3)])
    for name in ("np", "nu", "nv", "nk"):
        loads[name].wait()
    take_ghosts(0)
    for i in range(4):
        arrived(to_up[i][1], ni_recv.at[0, i], ~first)
        arrived(to_down[i][1], ni_recv.at[1, i], ~last)
    nest_first(0)
    nest_second(1)
    pass_ghosts(1)
    nest_arrived(2)
    nest_first(2)
    take_ghosts(1)
    nest_second(3)
    start_feedback(0)
    nest_arrived(4)
    nest_first(4)
    nest_second(5)
    start_feedback(1)
    outs = []

    def store(src, dst):
        outs.append(pltpu.make_async_copy(src, dst, out_sem.at[len(outs)]))
        outs[-1].start()
    store(n_p.at[6, pl.ds(2, 3)], p_out.at[1])
    store(n_u.at[pl.ds(2, 3)], u_out.at[1])
    store(n_v.at[pl.ds(1, 3)], v_out.at[1])
    pass_feedback(0)
    take_feedback(0, parent_rows[1], parent_rows[1])
    parent_exchange(1, parent_rows[1])
    pass_feedback(1)
    parent_substep(1)
    store(p_u.at[pl.ds(1, 3)], u_out.at[0])
    store(p_v, v_out.at[0])
    take_feedback(1, parent_rows[2], p_out.at[0])
    for wait in finish:
        wait()
    for copy in outs:
        copy.wait()


def put_out(p, u, v, p_out, u_out, v_out, sem):
    copies = [pltpu.make_async_copy(a, b, sem.at[i]) for i, (a, b) in enumerate(((p, p_out), (u, u_out), (v, v_out)))]
    for copy in copies:
        copy.start()
    for copy in copies:
        copy.wait()


def per_device(n, tiles, pressure, u_wind, v_wind, stiffness, vertical, nest_row0, nest_col0):
    fields = [jnp.transpose(x, (0, 2, 1, 3)) for x in (pressure, u_wind, v_wind, stiffness)]
    fields = [pltpu.with_memory_space_constraint(x, pltpu.HBM) for x in fields]
    _, rows, levels, cols = fields[0].shape
    win = cols // RATIO
    row = (levels, cols)
    owners = (LAST_X0 + n) // RATIO + 1
    a_count = owners - (1 + n) // RATIO
    b_count = (LAST_X0 - 1) // RATIO + 1
    vmem = lambda *shape: pltpu.VMEM(shape, F32)
    dma = lambda *shape: pltpu.SemaphoreType.DMA(shape)
    outs = pl.pallas_call(
        functools.partial(kernel, n, tiles),
        out_shape=[pltpu.VMEM((2, rows) + row, F32)] * 3,
        in_specs=[pl.BlockSpec(memory_space=pltpu.SMEM)] * 2
        + [pl.BlockSpec(memory_space=pltpu.VMEM)]
        + [pl.BlockSpec(memory_space=pl.ANY)] * 4,
        out_specs=[pl.BlockSpec(memory_space=pltpu.VMEM)] * 3,
        scratch_shapes=[
            vmem(7, 7, *row), vmem(6, *row), vmem(5, *row), vmem(5, *row),
            vmem(3, 5, *row), vmem(4, *row), vmem(3, *row), vmem(3, *row),
            vmem(OUTER, 8, 128), vmem(OUTER, 8, 128), vmem(OUTER, levels, win), vmem(OUTER, levels, win),
            vmem(OUTER, levels, win), vmem(*row), vmem(*row), vmem(3, 2, levels, 128),
            pltpu.VMEM((cols, win), BF16), pltpu.VMEM((levels, 6 * levels), BF16),
            *[vmem(8, 8, 128)] * 4,
            *[vmem(a_count, levels, win)] * 2, *[vmem(b_count, levels, win)] * 2,
            *[vmem(8, levels, win)] * 2, *[vmem(10, levels, win)] * 2,
            dma(8), dma(5), dma(2, 4), dma(2, 4), dma(2, 2, 2), dma(2, 2, 2), dma(2, 2), dma(2, 2), dma(2, 3), dma(2, 3),
            dma(OUTER, 12), dma(OUTER, 8), dma(OUTER, 7), dma(OUTER), dma(OUTER, 2), dma(OUTER, 2),
            dma(OUTER, 7), dma(OUTER), dma(OUTER, 8), dma(OUTER, 10),
        ],
        compiler_params=pltpu.CompilerParams(has_side_effects=True, vmem_limit_bytes=48 * 1024 * 1024),
        cost_estimate=pl.CostEstimate(flops=300_000_000, bytes_accessed=4_200_000, transcendentals=0),
    )(nest_row0, nest_col0, vertical, *fields)
    outs = pl.pallas_call(
        put_out,
        out_shape=[jax.ShapeDtypeStruct((2, rows) + row, F32)] * 3,
        in_specs=[pl.BlockSpec(memory_space=pltpu.VMEM)] * 3,
        out_specs=[pl.BlockSpec(memory_space=pl.ANY)] * 3,
        scratch_shapes=[dma(3)],
    )(*[pltpu.with_memory_space_constraint(x, pltpu.VMEM) for x in outs])
    return tuple(jnp.transpose(x, (0, 2, 1, 3)) for x in outs)


def solution(mesh):
    spec = P(None, None, ("grp", "tile"), None)
    tiles = mesh.shape["tile"]
    return jax.shard_map(
        functools.partial(per_device, mesh.shape["grp"] * tiles, tiles),
        mesh=mesh,
        in_specs=(spec, spec, spec, spec, P(), P(), P()),
        out_specs=(spec, spec, spec),
        check_vma=False,
    )
```

```python
import functools

import jax
import jax.numpy as jnp
from jax import lax
from jax.experimental import pallas as pl
from jax.experimental.pallas import tpu as pltpu
from jax.sharding import PartitionSpec as P

RATIO = 3
OUTER = 2
BLOCKS = 3
COURANT = 0.3
MIXING = 0.15
LAST_X0 = 60
GROUP = 6
MESH = pl.DeviceIdType.MESH
F32 = jnp.float32
BF16 = jnp.bfloat16


def pieces(x):
    a = x.astype(BF16)
    rest = x - a.astype(F32)
    b = rest.astype(BF16)
    c = (rest - b.astype(F32)).astype(BF16)
    return a, b, c


def kernel(
    n, tiles, lead,
    row0_in, col0_in, vert_in, p_in, u_in, v_in, k_in,
    p_out, u_out, v_out,
    n_p, n_u, n_v, n_k, p_p, p_u, p_v, p_k,
    g_send, g_recv, a_send, a_recv, b_send, b_recv, a_row, b_row, edge, f_send, f_recv, fold, mix,
    row0_ref, col0_ref, vert_ref,
    in_sem, out_sem, ni_send, ni_recv, nx_send, nx_recv, nm_send, nm_recv, px_send, px_recv,
    gs_send, gs_recv, e_send, a_sems, b_sems, f_sends, f_recvs,
):
    levels, cols = n_k.shape[1], n_k.shape[2]
    win = cols // RATIO
    me = lax.axis_index("grp") * tiles + lax.axis_index("tile")
    first, last = me == 0, me == n - 1
    own = RATIO * me
    finish = []

    def dev(d):
        d = d + 0 * me
        return (d // tiles, d % tiles)

    def remote(src, dst, s_sem, r_sem, to):
        return pltpu.make_async_remote_copy(
            src_ref=src, dst_ref=dst, send_sem=s_sem, recv_sem=r_sem, device_id=dev(to), device_id_type=MESH
        )

    def loop(low, high, body):
        lax.fori_loop(low, high, lambda i, _: (body(i), 0)[1], 0)

    def rows_of(count, body):
        for i in range(count):
            body(i)

    def arrived(ref, sem, cond=True):
        @pl.when(cond)
        def _():
            pltpu.make_async_copy(ref, ref, sem).wait()

    small = [
        pltpu.make_async_copy(src, dst, in_sem.at[8 + i])
        for i, (src, dst) in enumerate(((row0_in, row0_ref), (col0_in, col0_ref), (vert_in, vert_ref)))
    ]
    for copy in small:
        copy.start()
    loads = {}
    for at, (name, src, g, dst) in enumerate((
        ("pp", p_in, 0, p_p.at[0, pl.ds(1, 3)]), ("pv", v_in, 0, p_v), ("pu", u_in, 0, p_u.at[pl.ds(1, 3)]),
        ("np", p_in, 1, n_p.at[0, pl.ds(2, 3)]), ("nu", u_in, 1, n_u.at[pl.ds(2, 3)]),
        ("nv", v_in, 1, n_v.at[pl.ds(1, 3)]), ("nk", k_in, 1, n_k.at[pl.ds(1, 3)]), ("pk", k_in, 0, p_k),
    )):
        loads[name] = pltpu.make_async_copy(src.at[g], dst, in_sem.at[at])
        loads[name].start()

    ghosts_from, ghosts_to = g_recv.shape[1], GROUP + 4
    backs_to, backs_from = f_sends.shape[1], f_recv.shape[1]

    def ghost_to(k):
        d = own - lead + k - GROUP
        return d, (d >= 0) & (d < n), me - (d + lead + 2) // RATIO + 1

    def ghost_from(i):
        e = (me + lead + 2) // RATIO - 1 + i
        return e, (e >= 0) & (RATIO * e <= lead + me + GROUP)

    def back_to(i):
        e = (me + lead) // RATIO + i
        return e, RATIO * e < lead + me + GROUP, jnp.clip(me + lead - RATIO * e + GROUP - 1, 0, backs_from - 1)

    def back_from(k):
        d = own - lead + k - GROUP + 1
        return d, (d >= 0) & (d < n)

    a_from = tuple(range((lead + n) // RATIO, (lead + n + GROUP - 1) // RATIO + 1))
    b_from = tuple(range((lead - 1) // RATIO, (lead + GROUP - 2) // RATIO + 1))

    bar = pltpu.get_barrier_semaphore()
    count = jnp.where(first | last, 1, 2)

    def hello(d, cond):
        @pl.when(cond)
        def _():
            pl.semaphore_signal(bar, inc=1, device_id=dev(d), device_id_type=MESH)
    hello(me + 1, ~last)
    hello(me - 1, ~first)
    for i in range(ghosts_from):
        e, cond = ghost_from(i)
        hello(e, cond & (e != me))
    for k in range(ghosts_to):
        d, cond, _ = ghost_to(k)
        count = count + jnp.where(cond & (d != me), 1, 0)
    for k in range(backs_from):
        d, cond = back_from(k)
        hello(d, cond & (d != me))
    for i in range(backs_to):
        e, cond, _ = back_to(i)
        count = count + jnp.where(cond & (e != me), 1, 0)
    for e in a_from:
        hello(e, last)
        count = count + jnp.where(me == e, 1, 0)
    for e in b_from:
        if e > 0:
            hello(e, first)
            count = count + jnp.where(me == e, 1, 0)
    pl.semaphore_wait(bar, count)

    def parent_copies(s, rows):
        return (
            (remote(rows.at[2], p_p.at[s, 0], px_send.at[s, 0], px_recv.at[s, 0], me + 1), ~last),
            (remote(rows.at[0], p_p.at[s, 4], px_send.at[s, 1], px_recv.at[s, 1], me - 1), ~first),
        )

    to_up = (
        (p_in.at[1, 2], n_p.at[0, 1], nx_send.at[0, 0, 1], nx_recv.at[0, 0, 1]),
        (p_in.at[1, 1], n_p.at[0, 0], nx_send.at[0, 0, 0], nx_recv.at[0, 0, 0]),
        (u_in.at[1, pl.ds(1, 2)], n_u.at[pl.ds(0, 2)], ni_send.at[0, 0], ni_recv.at[0, 0]),
        (v_in.at[1, 2], n_v.at[0], ni_send.at[0, 1], ni_recv.at[0, 1]),
        (k_in.at[1, 2], n_k.at[0], ni_send.at[0, 2], ni_recv.at[0, 2]),
        (u_in.at[0, 2], p_u.at[0], px_send.at[0, 2], px_recv.at[0, 2]),
    )
    to_down = (
        (p_in.at[1, 0], n_p.at[0, 5], nx_send.at[0, 1, 0], nx_recv.at[0, 1, 0]),
        (p_in.at[1, 1], n_p.at[0, 6], nx_send.at[0, 1, 1], nx_recv.at[0, 1, 1]),
        (u_in.at[1, 0], n_u.at[5], ni_send.at[1, 0], ni_recv.at[1, 0]),
        (v_in.at[1, 0], n_v.at[4], ni_send.at[1, 1], ni_recv.at[1, 1]),
        (k_in.at[1, 0], n_k.at[4], ni_send.at[1, 2], ni_recv.at[1, 2]),
    )
    for i in range(6):
        for group, to, cond in ((to_up, me + 1, ~last), (to_down, me - 1, ~first)):
            if i < len(group):
                copy = remote(*group[i], to)
                pl.when(cond)(copy.start)
                finish.append(lambda copy=copy, cond=cond: pl.when(cond)(copy.wait_send))
    for copy, cond in parent_copies(0, p_in.at[0]):
        pl.when(cond)(copy.start)

    for copy in small:
        copy.wait()
    x0, y0 = row0_ref[0], col0_ref[0]
    rest = x0 - lead
    lane = lax.broadcasted_iota(jnp.int32, (levels, cols), 1)
    lane128 = lax.broadcasted_iota(jnp.int32, (levels, 128), 1)
    level128 = lax.broadcasted_iota(jnp.int32, (levels, 128), 0)
    row8 = lax.broadcasted_iota(jnp.int32, (8, 128), 0)

    def ghost_copy(o, k):
        d, cond, slot = ghost_to(k)
        return remote(g_send.at[o], g_recv.at[o, slot], gs_send.at[o, k], gs_recv.at[o, slot], d), cond & (d != me)

    def row_copies(o):
        for i, e in enumerate(a_from):
            yield remote(a_send.at[o], a_recv.at[o, i], e_send.at[o, 0], a_sems.at[o, i], n - 1), me == e
        for i, e in enumerate(b_from):
            if e > 0:
                yield remote(b_send.at[o], b_recv.at[o, i], e_send.at[o, 1], b_sems.at[o, i], 0), me == e

    def start_ghosts(o):
        pp, pu = p_p.at[o, pl.ds(1, 3)], p_u.at[pl.ds(1, 3)]

        def gather(j, total):
            right = jnp.sum(jnp.where(lane == y0 + win, pp[j], 0.0), axis=1, keepdims=True)
            left = jnp.sum(jnp.where(lane == y0 - 1, p_v[j], 0.0), axis=1, keepdims=True)
            both = jnp.where(level128 == lane128, right, 0.0) + jnp.where(level128 == lane128 - levels, left, 0.0)
            return jnp.where(row8 == j, jnp.sum(both, axis=0, keepdims=True), total)
        g_send[o] = lax.fori_loop(0, RATIO, gather, jnp.zeros((8, 128), F32))

        def column(k):
            d, cond, slot = ghost_to(k)

            @pl.when(cond & (d == me))
            def _():
                g_recv[o, slot] = g_send[o]
            copy, cond = ghost_copy(o, k)
            pl.when(cond)(copy.start)
        loop(0, ghosts_to, column)

        def pick_row(field, target):
            out = jnp.zeros((levels, cols), F32)
            for j in range(RATIO):
                out = jnp.where(target == own + j, field[j], out)
            return pltpu.roll(out, cols - y0, axis=1)[:, :win]

        @pl.when((me >= a_from[0]) & (me <= a_from[-1]))
        def _():
            a_send[o] = pick_row(pp, x0 + n)

        @pl.when((me >= b_from[0]) & (me <= b_from[-1]))
        def _():
            b_send[o] = pick_row(pu, x0 - 1)
        if b_from[0] == 0:
            @pl.when(first)
            def _():
                b_recv[o, 0] = b_send[o]
        for copy, cond in row_copies(o):
            pl.when(cond)(copy.start)

    def end_ghosts(o):
        def column(k):
            copy, cond = ghost_copy(o, k)
            pl.when(cond)(copy.wait_send)
        loop(0, ghosts_to, column)
        for copy, cond in row_copies(o):
            pl.when(cond)(copy.wait_send)

    def take_ghosts(o):
        for i in range(ghosts_from):
            e, cond = ghost_from(i)
            arrived(g_recv.at[o, i], gs_recv.at[o, i], cond & (e != me))
        for t in range(3):
            place = (me + lead + 2) % RATIO + rest + t
            row = jnp.zeros((1, 128), F32)
            for i in range(ghosts_from):
                row = row + jnp.sum(jnp.where(row8 == place - RATIO * i, g_recv[o, i], 0.0), axis=0, keepdims=True)
            right = jnp.sum(jnp.where(level128 == lane128, row, 0.0), axis=1, keepdims=True)
            left = jnp.sum(jnp.where(level128 == lane128 - levels, row, 0.0), axis=1, keepdims=True)
            edge[o, t, 0] = jnp.broadcast_to(right, (levels, 128))
            edge[o, t, 1] = jnp.broadcast_to(left, (levels, 128))

        @pl.when(first | last)
        def _():
            a = b = jnp.zeros((levels, win), F32)
            for i, e in enumerate(a_from):
                arrived(a_recv.at[o, i], a_sems.at[o, i], last)
                a = jnp.where((x0 + n >= RATIO * e) & (x0 + n < RATIO * (e + 1)), a_recv[o, i], a)
            for i, e in enumerate(b_from):
                if e > 0:
                    arrived(b_recv.at[o, i], b_sems.at[o, i], first)
                b = jnp.where((x0 - 1 >= RATIO * e) & (x0 - 1 < RATIO * (e + 1)), b_recv[o, i], b)
            x = jnp.where(jnp.broadcast_to(last.astype(jnp.int32), a.shape) > 0, a, b)
            wide = lax.dot_general(
                jnp.concatenate(pieces(x), axis=0), fold[...], (((1,), (1,)), ((), ())), preferred_element_type=F32
            )
            wide = (wide[:levels] + wide[levels:2 * levels]) + wide[2 * levels:]
            a_row[o] = wide
            b_row[o] = wide

    def from_right(x, ghost):
        moved = pltpu.roll(x, cols - 1, axis=1)
        if ghost is None:
            return moved
        tail = jnp.where(lane128 == 127, ghost, moved[:, cols - 128:])
        return jnp.concatenate([moved[:, :cols - 128], tail], axis=1)

    def from_left(x, ghost):
        moved = pltpu.roll(x, 1, axis=1)
        if ghost is None:
            return moved
        head = jnp.where(lane128 == 0, ghost, moved[:, :128])
        return jnp.concatenate([head, moved[:, 128:]], axis=1)

    def new_pressure(p, k, u, below, v, left):
        q = p - COURANT * k * ((u - below) + (v - from_left(v, left)))
        a = q.astype(BF16)
        b = (q - a.astype(F32)).astype(BF16)
        return q + jnp.dot(mix[...], jnp.concatenate([a, b, a], axis=0), preferred_element_type=F32)

    def nest_u(s, i):
        n_u[i] = n_u[i] - COURANT * (n_p[s, i + 1] - n_p[s, i])

    def nest_v(s, o, i, t):
        p = n_p[s, i + 1]
        v = n_v[i] - COURANT * (from_right(p, edge[o, t, 0]) - p)
        n_v[i] = v
        return p, v

    def below_nest(o):
        @pl.when(first)
        def _():
            n_u[1] = b_row[o]

    def above_nest(s, o):
        @pl.when(last)
        def _():
            n_p[s, 5] = a_row[o]

    def nest_row(s, o, i, t):
        p, v = nest_v(s, o, i, t)
        n_p[s + 1, i + 1] = new_pressure(p, n_k[i], n_u[i + 1], n_u[i], v, edge[o, t, 1])

    def middle_copies(blk):
        s = 2 * blk + 1
        return (
            (remote(n_p.at[s, 3], n_p.at[s, 0], nm_send.at[blk, 0], nm_recv.at[blk, 0], me + 1), ~last),
            (remote(n_p.at[s, 3], n_p.at[s, 6], nm_send.at[blk, 1], nm_recv.at[blk, 1], me - 1), ~first),
        )

    def end_copies(blk):
        s, nxt = 2 * blk + 2, blk + 1
        up = [remote(n_p.at[s, i + 3], n_p.at[s, i], nx_send.at[nxt, 0, i], nx_recv.at[nxt, 0, i], me + 1) for i in range(2)]
        down = [remote(n_p.at[s, i + 2], n_p.at[s, i + 5], nx_send.at[nxt, 1, i], nx_recv.at[nxt, 1, i], me - 1) for i in range(2)]
        return up, down

    def nest_block(blk):
        s = 2 * blk
        before, after = blk // 2, (blk + 1) // 2
        for i in range(2):
            arrived(n_p.at[s, i], nx_recv.at[blk, 0, i], ~first)
            arrived(n_p.at[s, 5 + i], nx_recv.at[blk, 1, i], ~last)

        @pl.when(blk > 0)
        def _():
            arrived(n_p.at[s - 1, 0], nm_recv.at[blk - 1, 0], ~first)
            arrived(n_p.at[s - 1, 6], nm_recv.at[blk - 1, 1], ~last)
            nest_u(s - 1, 0)
            nest_u(s - 1, 5)
        pl.when(blk < 2)(lambda: take_ghosts(blk))

        above_nest(s, before)
        for i in range(6):
            nest_u(s, i)
        below_nest(before)
        for i in (2, 1, 3, 4, 0):
            nest_row(s, before, i, (i + 2) // RATIO)

        @pl.when(blk < BLOCKS - 1)
        def _():
            for copy, cond in middle_copies(blk):
                pl.when(cond)(copy.start)

        above_nest(s + 1, after)
        for i in range(1, 5):
            nest_u(s + 1, i)
        below_nest(after)
        up, down = end_copies(blk)
        more = blk < BLOCKS - 1
        nest_row(s + 1, after, 2, 1)
        pl.when(more & ~last)(up[0].start)
        pl.when(more & ~first)(down[1].start)
        nest_row(s + 1, after, 3, 1)
        pl.when(more & ~last)(up[1].start)
        nest_row(s + 1, after, 1, 1)
        pl.when(more & ~first)(down[0].start)

        @pl.when(more)
        def _():
            nest_v(s + 1, after, 0, 0)
            nest_v(s + 1, after, 4, 2)

    def parent_substep(s):
        arrived(p_p.at[s, 0], px_recv.at[s, 0], ~first)
        arrived(p_p.at[s, 4], px_recv.at[s, 1], ~last)
        for i in range(4):
            p_u[i] = p_u[i] - COURANT * (p_p[s, i + 1] - p_p[s, i])

        @pl.when(first)
        def _():
            p_u[0] = jnp.zeros((levels, cols), F32)

        @pl.when(last)
        def _():
            p_u[3] = jnp.zeros((levels, cols), F32)

        def row(r):
            p = p_p[s, r + 1]
            v = p_v[r] - COURANT * (from_right(p, None) - p)
            p_v[r] = v
            p_p[s + 1, r + 1] = new_pressure(p, p_k[r], p_u[r + 1], p_u[r], v, None)
        rows_of(RATIO, row)

    def back_copy(o, i):
        e, cond, slot = back_to(i)
        return remote(f_send.at[o], f_recv.at[o, slot], f_sends.at[o, i], f_recvs.at[o, slot], e), cond & (e != me)

    def start_feedback(o):
        rows = n_p.at[3 * (o + 1)]
        stack = jnp.concatenate(pieces((rows[2] + rows[3]) + rows[4]), axis=0)
        mean = jnp.dot(stack, fold[...], preferred_element_type=F32)
        f_send[o] = ((mean[:levels] + mean[levels:2 * levels]) + mean[2 * levels:]) * (1.0 / (RATIO * RATIO))
        for i in range(backs_to):
            e, cond, slot = back_to(i)

            @pl.when(cond & (e == me))
            def _():
                f_recv[o, slot] = f_send[o]
            copy, cond = back_copy(o, i)
            pl.when(cond)(copy.start)

    def take_feedback(o, target):
        for k in range(backs_from):
            d, cond = back_from(k)
            arrived(f_recv.at[o, k], f_recvs.at[o, k], cond & (d != me))
        under = (lane >= y0) & (lane < y0 + win)

        def place(j):
            row = own + j
            value = f_recv[o, j + GROUP - 1]
            for i in range(1, GROUP):
                value = jnp.where(rest == i, f_recv[o, j + GROUP - 1 - i], value)
            value = pltpu.roll(jnp.concatenate([value, jnp.zeros((levels, cols - win), F32)], axis=1), y0, axis=1)
            inside = ((row >= x0) & (row < x0 + n)).astype(jnp.int32)
            target[j] = jnp.where(under & (jnp.broadcast_to(inside, (levels, cols)) > 0), value, p_p[o + 1, j + 1])
        loop(0, RATIO, place)

    for name in ("pp", "pv", "pu"):
        loads[name].wait()
    spot = lax.broadcasted_iota(jnp.int32, (cols, win), 0) - RATIO * lax.broadcasted_iota(jnp.int32, (cols, win), 1)

    def stores():
        pairs = (
            (n_p.at[6, pl.ds(2, 3)], p_out.at[1]), (n_u.at[pl.ds(2, 3)], u_out.at[1]), (n_v.at[pl.ds(1, 3)], v_out.at[1]),
            (p_u.at[pl.ds(1, 3)], u_out.at[0]), (p_v, v_out.at[0]),
        )
        return [pltpu.make_async_copy(src, dst, out_sem.at[i]) for i, (src, dst) in enumerate(pairs)]

    def turn(it):
        pl.when(it < OUTER)(lambda: start_ghosts(it))

        @pl.when(it == 0)
        def _():
            fold[...] = jnp.where((spot >= 0) & (spot < RATIO), 1.0, 0.0).astype(BF16)
            block = lax.broadcasted_iota(jnp.int32, (levels, 3 * levels), 1)
            copies = (block % levels == lax.broadcasted_iota(jnp.int32, (levels, 3 * levels), 0)).astype(F32)
            wide = jnp.dot(MIXING * vert_ref[...], copies, precision=lax.Precision.HIGHEST, preferred_element_type=F32)
            m1, m2, _ = (x.astype(F32) for x in pieces(wide))
            mix[...] = jnp.where(block >= 2 * levels, m2, m1).astype(BF16)
            for name in ("np", "nu", "nv", "nk", "pk"):
                loads[name].wait()
            for i in range(3):
                arrived(to_up[i + 2][1], ni_recv.at[0, i], ~first)
                arrived(to_down[i + 2][1], ni_recv.at[1, i], ~last)
            arrived(p_u.at[0], px_recv.at[0, 2], ~first)
        nest_block(it)
        pl.when(it > 0)(lambda: start_feedback(it - 1))

        @pl.when(it == 2)
        def _():
            take_feedback(0, p_p.at[1, pl.ds(1, 3)])
            for copy, cond in parent_copies(1, p_p.at[1, pl.ds(1, 3)]):
                pl.when(cond)(copy.start)
            for copy in stores()[:3]:
                copy.start()
        pl.when(it != 1)(lambda: parent_substep(it // 2))
    loop(0, BLOCKS, turn)
    outs = stores()
    for copy in outs[3:]:
        copy.start()
    take_feedback(1, p_out.at[0])

    for o in range(OUTER):
        end_ghosts(o)
        for i in range(backs_to):
            copy, cond = back_copy(o, i)
            pl.when(cond)(copy.wait_send)
    for blk in range(BLOCKS - 1):
        for copy, cond in middle_copies(blk):
            pl.when(cond)(copy.wait_send)
        up, down = end_copies(blk)
        for i in range(2):
            pl.when(~last)(up[i].wait_send)
            pl.when(~first)(down[i].wait_send)
    for s, rows in ((0, p_in.at[0]), (1, p_p.at[1, pl.ds(1, 3)])):
        for copy, cond in parent_copies(s, rows):
            pl.when(cond)(copy.wait_send)
    for wait in finish:
        wait()
    for copy in outs:
        copy.wait()


def put_out(p, u, v, p_out, u_out, v_out, sem):
    copies = [pltpu.make_async_copy(a, b, sem.at[i]) for i, (a, b) in enumerate(((p, p_out), (u, u_out), (v, v_out)))]
    for copy in copies:
        copy.start()
    for copy in copies:
        copy.wait()


def per_device(n, tiles, pressure, u_wind, v_wind, stiffness, vertical, nest_row0, nest_col0):
    fields = [jnp.transpose(x, (0, 2, 1, 3)) for x in (pressure, u_wind, v_wind, stiffness)]
    operands = [pltpu.with_memory_space_constraint(x, pltpu.HBM) for x in (nest_row0, nest_col0, vertical, *fields)]
    _, rows, levels, cols = fields[0].shape
    win = cols // RATIO
    row = (levels, cols)
    vmem = lambda *shape: pltpu.VMEM(shape, F32)
    dma = lambda *shape: pltpu.SemaphoreType.DMA(shape)

    owners = lambda rows, at: (at + rows - 1) // RATIO - at // RATIO + 1

    def most(rows):
        return max(owners(rows, at) for at in range(RATIO))

    def call(lead):
        return pl.pallas_call(
            functools.partial(kernel, n, tiles, lead),
            out_shape=[pltpu.VMEM((2, rows) + row, F32)] * 3,
            in_specs=[pl.BlockSpec(memory_space=pl.ANY)] * 7,
            out_specs=[pl.BlockSpec(memory_space=pltpu.VMEM)] * 3,
            scratch_shapes=[
                vmem(7, 7, *row), vmem(6, *row), vmem(5, *row), vmem(5, *row),
                vmem(3, 5, *row), vmem(4, *row), vmem(3, *row), vmem(3, *row),
                vmem(OUTER, 8, 128), vmem(OUTER, most(GROUP + 2), 8, 128), vmem(OUTER, levels, win), vmem(OUTER, most(GROUP), levels, win),
                vmem(OUTER, levels, win), vmem(OUTER, most(GROUP), levels, win), vmem(OUTER, *row), vmem(OUTER, *row),
                vmem(OUTER, 3, 2, levels, 128), vmem(OUTER, levels, win), vmem(OUTER, GROUP + 2, levels, win),
                pltpu.VMEM((cols, win), BF16), pltpu.VMEM((levels, 3 * levels), BF16),
                pltpu.SMEM(nest_row0.shape, jnp.int32), pltpu.SMEM(nest_col0.shape, jnp.int32), vmem(*vertical.shape),
                dma(11), dma(5), dma(2, 3), dma(2, 3), dma(3, 2, 2), dma(3, 2, 2), dma(2, 2), dma(2, 2), dma(2, 3), dma(2, 3),
                dma(OUTER, GROUP + 4), dma(OUTER, most(GROUP + 2)), dma(OUTER, 2), dma(OUTER, most(GROUP)), dma(OUTER, most(GROUP)),
                dma(OUTER, most(GROUP)), dma(OUTER, GROUP + 2),
            ],
            compiler_params=pltpu.CompilerParams(
                collective_id=lead // GROUP, has_side_effects=True, vmem_limit_bytes=48 * 1024 * 1024
            ),
            cost_estimate=pl.CostEstimate(flops=300_000_000, bytes_accessed=4_200_000, transcendentals=0),
        )
    branches = [lambda *args, lead=lead: tuple(call(lead)(*args)) for lead in range(1, LAST_X0 + 1, GROUP)]
    outs = lax.switch((nest_row0[0] - 1) // GROUP, branches, *operands)
    outs = pl.pallas_call(
        put_out,
        out_shape=[jax.ShapeDtypeStruct((2, rows) + row, F32)] * 3,
        in_specs=[pl.BlockSpec(memory_space=pltpu.VMEM)] * 3,
        out_specs=[pl.BlockSpec(memory_space=pl.ANY)] * 3,
        scratch_shapes=[dma(3)],
    )(*[pltpu.with_memory_space_constraint(x, pltpu.VMEM) for x in outs])
    return tuple(jnp.transpose(x, (0, 2, 1, 3)) for x in outs)


def solution(mesh):
    spec = P(None, None, ("grp", "tile"), None)
    tiles = mesh.shape["tile"]
    return jax.shard_map(
        functools.partial(per_device, mesh.shape["grp"] * tiles, tiles),
        mesh=mesh,
        in_specs=(spec, spec, spec, spec, P(), P(), P()),
        out_specs=(spec, spec, spec),
        check_vma=False,
    )
```

```python
import functools

import jax
import jax.numpy as jnp
from jax import lax
from jax.experimental import pallas as pl
from jax.experimental.pallas import tpu as pltpu
from jax.sharding import PartitionSpec as P

RATIO = 3
OUTER = 2
BLOCKS = 3
COURANT = 0.3
MIXING = 0.15
LAST_X0 = 60
GROUP = 6
MESH = pl.DeviceIdType.MESH
F32 = jnp.float32
BF16 = jnp.bfloat16


def pieces(x):
    a = x.astype(BF16)
    rest = x - a.astype(F32)
    b = rest.astype(BF16)
    c = (rest - b.astype(F32)).astype(BF16)
    return a, b, c


def kernel(
    n, tiles, lead,
    row0_in, col0_in, vert_in, p_in, u_in, v_in, k_in,
    p_out, u_out, v_out,
    n_p, n_u, n_v, n_k, p_p, p_u, p_v, p_k,
    g_send, g_recv, a_send, a_recv, b_send, b_recv, a_row, b_row, edge, f_send, f_recv, fold, mix,
    row0_ref, col0_ref, vert_ref,
    in_sem, out_sem, ni_send, ni_recv, nx_send, nx_recv, nm_send, nm_recv, px_send, px_recv,
    gs_send, gs_recv, e_send, a_sems, b_sems, f_sends, f_recvs,
):
    levels, cols = n_k.shape[1], n_k.shape[2]
    win = cols // RATIO
    me = lax.axis_index("grp") * tiles + lax.axis_index("tile")
    first, last = me == 0, me == n - 1
    own = RATIO * me
    finish = []

    def dev(d):
        d = d + 0 * me
        return (d // tiles, d % tiles)

    def remote(src, dst, s_sem, r_sem, to):
        return pltpu.make_async_remote_copy(
            src_ref=src, dst_ref=dst, send_sem=s_sem, recv_sem=r_sem, device_id=dev(to), device_id_type=MESH
        )

    def loop(low, high, body):
        lax.fori_loop(low, high, lambda i, _: (body(i), 0)[1], 0)

    def rows_of(count, body):
        for i in range(count):
            body(i)

    def arrived(ref, sem, cond=True):
        @pl.when(cond)
        def _():
            pltpu.make_async_copy(ref, ref, sem).wait()

    small = [
        pltpu.make_async_copy(src, dst, in_sem.at[8 + i])
        for i, (src, dst) in enumerate(((row0_in, row0_ref), (col0_in, col0_ref), (vert_in, vert_ref)))
    ]
    for copy in small:
        copy.start()
    loads = {}
    for at, (name, src, g, dst) in enumerate((
        ("pp", p_in, 0, p_p.at[0, pl.ds(1, 3)]), ("pv", v_in, 0, p_v), ("pu", u_in, 0, p_u.at[pl.ds(1, 3)]),
        ("np", p_in, 1, n_p.at[0, pl.ds(2, 3)]), ("nu", u_in, 1, n_u.at[pl.ds(2, 3)]),
        ("nv", v_in, 1, n_v.at[pl.ds(1, 3)]), ("nk", k_in, 1, n_k.at[pl.ds(1, 3)]), ("pk", k_in, 0, p_k),
    )):
        loads[name] = pltpu.make_async_copy(src.at[g], dst, in_sem.at[at])
        loads[name].start()

    ghosts_from, ghosts_to = g_recv.shape[1], GROUP + 4
    backs_to, backs_from = f_sends.shape[1], f_recv.shape[1]

    def ghost_to(k):
        d = own - lead + k - GROUP
        return d, (d >= 0) & (d < n), me - (d + lead + 2) // RATIO + 1

    def ghost_from(i):
        e = (me + lead + 2) // RATIO - 1 + i
        return e, (e >= 0) & (RATIO * e <= lead + me + GROUP)

    def back_to(i):
        e = (me + lead) // RATIO + i
        return e, RATIO * e < lead + me + GROUP, jnp.clip(me + lead - RATIO * e + GROUP - 1, 0, backs_from - 1)

    def back_from(k):
        d = own - lead + k - GROUP + 1
        return d, (d >= 0) & (d < n)

    a_from = tuple(range((lead + n) // RATIO, (lead + n + GROUP - 1) // RATIO + 1))
    b_from = tuple(range((lead - 1) // RATIO, (lead + GROUP - 2) // RATIO + 1))

    bar = pltpu.get_barrier_semaphore()
    count = jnp.where(first | last, 1, 2)

    def hello(d, cond):
        @pl.when(cond)
        def _():
            pl.semaphore_signal(bar, inc=1, device_id=dev(d), device_id_type=MESH)
    hello(me + 1, ~last)
    hello(me - 1, ~first)
    for i in range(ghosts_from):
        e, cond = ghost_from(i)
        hello(e, cond & (e != me))
    for k in range(ghosts_to):
        d, cond, _ = ghost_to(k)
        count = count + jnp.where(cond & (d != me), 1, 0)
    for k in range(backs_from):
        d, cond = back_from(k)
        hello(d, cond & (d != me))
    for i in range(backs_to):
        e, cond, _ = back_to(i)
        count = count + jnp.where(cond & (e != me), 1, 0)
    for e in a_from:
        hello(e, last)
        count = count + jnp.where(me == e, 1, 0)
    for e in b_from:
        if e > 0:
            hello(e, first)
            count = count + jnp.where(me == e, 1, 0)
    pl.semaphore_wait(bar, count)

    def parent_u_copy():
        return remote(u_in.at[0, 2], p_u.at[0], px_send.at[0, 2], px_recv.at[0, 2], me + 1)

    def parent_copies(s, rows):
        return (
            (remote(rows.at[2], p_p.at[s, 0], px_send.at[s, 0], px_recv.at[s, 0], me + 1), ~last),
            (remote(rows.at[0], p_p.at[s, 4], px_send.at[s, 1], px_recv.at[s, 1], me - 1), ~first),
        )

    to_up = (
        (p_in.at[1, 2], n_p.at[0, 1], nx_send.at[0, 0, 1], nx_recv.at[0, 0, 1]),
        (p_in.at[1, 1], n_p.at[0, 0], nx_send.at[0, 0, 0], nx_recv.at[0, 0, 0]),
        (u_in.at[1, pl.ds(1, 2)], n_u.at[pl.ds(0, 2)], ni_send.at[0, 0], ni_recv.at[0, 0]),
        (v_in.at[1, 2], n_v.at[0], ni_send.at[0, 1], ni_recv.at[0, 1]),
        (k_in.at[1, 2], n_k.at[0], ni_send.at[0, 2], ni_recv.at[0, 2]),
    )
    to_down = (
        (p_in.at[1, 0], n_p.at[0, 5], nx_send.at[0, 1, 0], nx_recv.at[0, 1, 0]),
        (p_in.at[1, 1], n_p.at[0, 6], nx_send.at[0, 1, 1], nx_recv.at[0, 1, 1]),
        (u_in.at[1, 0], n_u.at[5], ni_send.at[1, 0], ni_recv.at[1, 0]),
        (v_in.at[1, 0], n_v.at[4], ni_send.at[1, 1], ni_recv.at[1, 1]),
        (k_in.at[1, 0], n_k.at[4], ni_send.at[1, 2], ni_recv.at[1, 2]),
    )
    for i in range(5):
        for group, to, cond in ((to_up, me + 1, ~last), (to_down, me - 1, ~first)):
            if i < len(group):
                copy = remote(*group[i], to)
                pl.when(cond)(copy.start)
                finish.append(lambda copy=copy, cond=cond: pl.when(cond)(copy.wait_send))

    for copy in small:
        copy.wait()
    x0, y0 = row0_ref[0], col0_ref[0]
    rest = x0 - lead
    lane = lax.broadcasted_iota(jnp.int32, (levels, cols), 1)
    lane128 = lax.broadcasted_iota(jnp.int32, (levels, 128), 1)
    level128 = lax.broadcasted_iota(jnp.int32, (levels, 128), 0)
    row8 = lax.broadcasted_iota(jnp.int32, (8, 128), 0)

    def ghost_copy(o, k):
        d, cond, slot = ghost_to(k)
        return remote(g_send.at[o], g_recv.at[o, slot], gs_send.at[o, k], gs_recv.at[o, slot], d), cond & (d != me)

    def row_copies(o):
        for i, e in enumerate(a_from):
            yield remote(a_send.at[o], a_recv.at[o, i], e_send.at[o, 0], a_sems.at[o, i], n - 1), me == e
        for i, e in enumerate(b_from):
            if e > 0:
                yield remote(b_send.at[o], b_recv.at[o, i], e_send.at[o, 1], b_sems.at[o, i], 0), me == e

    def start_ghosts(o):
        pp, pu = p_p.at[o, pl.ds(1, 3)], p_u.at[pl.ds(1, 3)]

        def gather(j, total):
            right = jnp.sum(jnp.where(lane == y0 + win, pp[j], 0.0), axis=1, keepdims=True)
            left = jnp.sum(jnp.where(lane == y0 - 1, p_v[j], 0.0), axis=1, keepdims=True)
            both = jnp.where(level128 == lane128, right, 0.0) + jnp.where(level128 == lane128 - levels, left, 0.0)
            return jnp.where(row8 == j, jnp.sum(both, axis=0, keepdims=True), total)
        g_send[o] = lax.fori_loop(0, RATIO, gather, jnp.zeros((8, 128), F32))

        def column(k):
            d, cond, slot = ghost_to(k)

            @pl.when(cond & (d == me))
            def _():
                g_recv[o, slot] = g_send[o]
            copy, cond = ghost_copy(o, k)
            pl.when(cond)(copy.start)
        loop(0, ghosts_to, column)

        def pick_row(field, target):
            out = jnp.zeros((levels, cols), F32)
            for j in range(RATIO):
                out = jnp.where(target == own + j, field[j], out)
            return pltpu.roll(out, cols - y0, axis=1)[:, :win]

        @pl.when((me >= a_from[0]) & (me <= a_from[-1]))
        def _():
            a_send[o] = pick_row(pp, x0 + n)

        @pl.when((me >= b_from[0]) & (me <= b_from[-1]))
        def _():
            b_send[o] = pick_row(pu, x0 - 1)
        if b_from[0] == 0:
            @pl.when(first)
            def _():
                b_recv[o, 0] = b_send[o]
        for copy, cond in row_copies(o):
            pl.when(cond)(copy.start)

    def end_ghosts(o):
        def column(k):
            copy, cond = ghost_copy(o, k)
            pl.when(cond)(copy.wait_send)
        loop(0, ghosts_to, column)
        for copy, cond in row_copies(o):
            pl.when(cond)(copy.wait_send)

    def take_ghosts(o):
        for i in range(ghosts_from):
            e, cond = ghost_from(i)
            arrived(g_recv.at[o, i], gs_recv.at[o, i], cond & (e != me))
        for t in range(3):
            place = (me + lead + 2) % RATIO + rest + t
            row = jnp.zeros((1, 128), F32)
            for i in range(ghosts_from):
                row = row + jnp.sum(jnp.where(row8 == place - RATIO * i, g_recv[o, i], 0.0), axis=0, keepdims=True)
            right = jnp.sum(jnp.where(level128 == lane128, row, 0.0), axis=1, keepdims=True)
            left = jnp.sum(jnp.where(level128 == lane128 - levels, row, 0.0), axis=1, keepdims=True)
            edge[o, t, 0] = jnp.broadcast_to(right, (levels, 128))
            edge[o, t, 1] = jnp.broadcast_to(left, (levels, 128))

        @pl.when(first | last)
        def _():
            a = b = jnp.zeros((levels, win), F32)
            for i, e in enumerate(a_from):
                arrived(a_recv.at[o, i], a_sems.at[o, i], last)
                a = jnp.where((x0 + n >= RATIO * e) & (x0 + n < RATIO * (e + 1)), a_recv[o, i], a)
            for i, e in enumerate(b_from):
                if e > 0:
                    arrived(b_recv.at[o, i], b_sems.at[o, i], first)
                b = jnp.where((x0 - 1 >= RATIO * e) & (x0 - 1 < RATIO * (e + 1)), b_recv[o, i], b)
            x = jnp.where(jnp.broadcast_to(last.astype(jnp.int32), a.shape) > 0, a, b)
            wide = lax.dot_general(
                jnp.concatenate(pieces(x), axis=0), fold[...], (((1,), (1,)), ((), ())), preferred_element_type=F32
            )
            wide = (wide[:levels] + wide[levels:2 * levels]) + wide[2 * levels:]
            a_row[o] = wide
            b_row[o] = wide

    def from_right(x, ghost):
        moved = pltpu.roll(x, cols - 1, axis=1)
        if ghost is None:
            return moved
        tail = jnp.where(lane128 == 127, ghost, moved[:, cols - 128:])
        return jnp.concatenate([moved[:, :cols - 128], tail], axis=1)

    def from_left(x, ghost):
        moved = pltpu.roll(x, 1, axis=1)
        if ghost is None:
            return moved
        head = jnp.where(lane128 == 0, ghost, moved[:, :128])
        return jnp.concatenate([head, moved[:, 128:]], axis=1)

    def new_pressure(p, k, u, below, v, left):
        q = p - COURANT * k * ((u - below) + (v - from_left(v, left)))
        a = q.astype(BF16)
        b = (q - a.astype(F32)).astype(BF16)
        return q + jnp.dot(mix[...], jnp.concatenate([a, b, a], axis=0), preferred_element_type=F32)

    def nest_u(s, i):
        n_u[i] = n_u[i] - COURANT * (n_p[s, i + 1] - n_p[s, i])

    def nest_v(s, o, i, t):
        p = n_p[s, i + 1]
        v = n_v[i] - COURANT * (from_right(p, edge[o, t, 0]) - p)
        n_v[i] = v
        return p, v

    def below_nest(o):
        @pl.when(first)
        def _():
            n_u[1] = b_row[o]

    def above_nest(s, o):
        @pl.when(last)
        def _():
            n_p[s, 5] = a_row[o]

    def nest_row(s, o, i, t):
        p, v = nest_v(s, o, i, t)
        n_p[s + 1, i + 1] = new_pressure(p, n_k[i], n_u[i + 1], n_u[i], v, edge[o, t, 1])

    def middle_copies(blk):
        s = 2 * blk + 1
        return (
            (remote(n_p.at[s, 3], n_p.at[s, 0], nm_send.at[blk, 0], nm_recv.at[blk, 0], me + 1), ~last),
            (remote(n_p.at[s, 3], n_p.at[s, 6], nm_send.at[blk, 1], nm_recv.at[blk, 1], me - 1), ~first),
        )

    def end_copies(blk):
        s, nxt = 2 * blk + 2, blk + 1
        up = [remote(n_p.at[s, i + 3], n_p.at[s, i], nx_send.at[nxt, 0, i], nx_recv.at[nxt, 0, i], me + 1) for i in range(2)]
        down = [remote(n_p.at[s, i + 2], n_p.at[s, i + 5], nx_send.at[nxt, 1, i], nx_recv.at[nxt, 1, i], me - 1) for i in range(2)]
        return up, down

    def nest_block(blk):
        s = 2 * blk
        before, after = blk // 2, (blk + 1) // 2
        more = blk < BLOCKS - 1
        up, down = end_copies(blk)

        pl.when(blk == 0)(lambda: take_ghosts(0))
        for i in (2, 3):
            nest_u(s, i)
        nest_row(s, before, 2, 1)

        @pl.when(more)
        def _():
            for copy, cond in middle_copies(blk):
                pl.when(cond)(copy.start)

        @pl.when(blk > 0)
        def _():
            arrived(n_p.at[s - 1, 0], nm_recv.at[blk - 1, 0], ~first)
            arrived(n_p.at[s - 1, 6], nm_recv.at[blk - 1, 1], ~last)
            nest_u(s - 1, 0)
            nest_u(s - 1, 5)
        for i in range(2):
            arrived(n_p.at[s, i], nx_recv.at[blk, 0, i], ~first)
            arrived(n_p.at[s, 5 + i], nx_recv.at[blk, 1, i], ~last)

        @pl.when(blk == 0)
        def _():
            for i in range(3):
                arrived(to_up[i + 2][1], ni_recv.at[0, i], ~first)
                arrived(to_down[i + 2][1], ni_recv.at[1, i], ~last)
        above_nest(s, before)
        for i in (0, 1, 4, 5):
            nest_u(s, i)
        below_nest(before)
        nest_row(s, before, 3, 1)
        nest_row(s, before, 1, 1)
        pl.when(blk == 1)(lambda: take_ghosts(1))

        for i in (2, 3):
            nest_u(s + 1, i)
        nest_row(s + 1, after, 2, 1)
        pl.when(more & ~last)(up[0].start)
        pl.when(more & ~first)(down[1].start)
        nest_row(s, before, 4, 2)
        above_nest(s + 1, after)
        nest_u(s + 1, 4)
        nest_row(s + 1, after, 3, 1)
        pl.when(more & ~last)(up[1].start)
        nest_row(s, before, 0, 0)
        nest_u(s + 1, 1)
        below_nest(after)
        nest_row(s + 1, after, 1, 1)
        pl.when(more & ~first)(down[0].start)

        @pl.when(more)
        def _():
            nest_v(s + 1, after, 0, 0)
            nest_v(s + 1, after, 4, 2)

    def parent_substep(s):
        arrived(p_p.at[s, 0], px_recv.at[s, 0], ~first)
        arrived(p_p.at[s, 4], px_recv.at[s, 1], ~last)
        for i in range(4):
            p_u[i] = p_u[i] - COURANT * (p_p[s, i + 1] - p_p[s, i])

        @pl.when(first)
        def _():
            p_u[0] = jnp.zeros((levels, cols), F32)

        @pl.when(last)
        def _():
            p_u[3] = jnp.zeros((levels, cols), F32)

        def row(r):
            p = p_p[s, r + 1]
            v = p_v[r] - COURANT * (from_right(p, None) - p)
            p_v[r] = v
            p_p[s + 1, r + 1] = new_pressure(p, p_k[r], p_u[r + 1], p_u[r], v, None)
        rows_of(RATIO, row)

    def back_copy(o, i):
        e, cond, slot = back_to(i)
        return remote(f_send.at[o], f_recv.at[o, slot], f_sends.at[o, i], f_recvs.at[o, slot], e), cond & (e != me)

    def start_feedback(o):
        rows = n_p.at[3 * (o + 1)]
        stack = jnp.concatenate(pieces((rows[2] + rows[3]) + rows[4]), axis=0)
        mean = jnp.dot(stack, fold[...], preferred_element_type=F32)
        f_send[o] = ((mean[:levels] + mean[levels:2 * levels]) + mean[2 * levels:]) * (1.0 / (RATIO * RATIO))
        for i in range(backs_to):
            e, cond, slot = back_to(i)

            @pl.when(cond & (e == me))
            def _():
                f_recv[o, slot] = f_send[o]
            copy, cond = back_copy(o, i)
            pl.when(cond)(copy.start)

    def take_feedback(o, target):
        for k in range(backs_from):
            d, cond = back_from(k)
            arrived(f_recv.at[o, k], f_recvs.at[o, k], cond & (d != me))
        under = (lane >= y0) & (lane < y0 + win)

        def place(j):
            row = own + j
            value = f_recv[o, j + GROUP - 1]
            for i in range(1, GROUP):
                value = jnp.where(rest == i, f_recv[o, j + GROUP - 1 - i], value)
            value = pltpu.roll(jnp.concatenate([value, jnp.zeros((levels, cols - win), F32)], axis=1), y0, axis=1)
            inside = ((row >= x0) & (row < x0 + n)).astype(jnp.int32)
            target[j] = jnp.where(under & (jnp.broadcast_to(inside, (levels, cols)) > 0), value, p_p[o + 1, j + 1])
        loop(0, RATIO, place)

    for name in ("pp", "pv", "pu"):
        loads[name].wait()
    spot = lax.broadcasted_iota(jnp.int32, (cols, win), 0) - RATIO * lax.broadcasted_iota(jnp.int32, (cols, win), 1)

    def stores():
        pairs = (
            (n_p.at[6, pl.ds(2, 3)], p_out.at[1]), (n_u.at[pl.ds(2, 3)], u_out.at[1]), (n_v.at[pl.ds(1, 3)], v_out.at[1]),
            (p_u.at[pl.ds(1, 3)], u_out.at[0]), (p_v, v_out.at[0]),
        )
        return [pltpu.make_async_copy(src, dst, out_sem.at[i]) for i, (src, dst) in enumerate(pairs)]

    def turn(it):
        pl.when(it < OUTER)(lambda: start_ghosts(it))

        @pl.when(it == 0)
        def _():
            for copy, cond in parent_copies(0, p_in.at[0]):
                pl.when(cond)(copy.start)
            pl.when(~last)(parent_u_copy().start)

        @pl.when(it == 0)
        def _():
            fold[...] = jnp.where((spot >= 0) & (spot < RATIO), 1.0, 0.0).astype(BF16)
            block = lax.broadcasted_iota(jnp.int32, (levels, 3 * levels), 1)
            copies = (block % levels == lax.broadcasted_iota(jnp.int32, (levels, 3 * levels), 0)).astype(F32)
            wide = jnp.dot(MIXING * vert_ref[...], copies, precision=lax.Precision.HIGHEST, preferred_element_type=F32)
            m1, m2, _ = (x.astype(F32) for x in pieces(wide))
            mix[...] = jnp.where(block >= 2 * levels, m2, m1).astype(BF16)
            for name in ("np", "nu", "nv", "nk", "pk"):
                loads[name].wait()
        nest_block(it)

        @pl.when(it == 2)
        def _():
            take_feedback(0, p_p.at[1, pl.ds(1, 3)])
            for copy, cond in parent_copies(1, p_p.at[1, pl.ds(1, 3)]):
                pl.when(cond)(copy.start)
        pl.when(it > 0)(lambda: start_feedback(it - 1))

        @pl.when(it == 2)
        def _():
            for copy in stores()[:3]:
                copy.start()
        pl.when(it == 0)(lambda: arrived(p_u.at[0], px_recv.at[0, 2], ~first))
        pl.when(it != 1)(lambda: parent_substep(it // 2))
    loop(0, BLOCKS, turn)
    outs = stores()
    for copy in outs[3:]:
        copy.start()
    for o in range(OUTER):
        end_ghosts(o)
        for i in range(backs_to):
            copy, cond = back_copy(o, i)
            pl.when(cond)(copy.wait_send)
    for blk in range(BLOCKS - 1):
        for copy, cond in middle_copies(blk):
            pl.when(cond)(copy.wait_send)
        up, down = end_copies(blk)
        for i in range(2):
            pl.when(~last)(up[i].wait_send)
            pl.when(~first)(down[i].wait_send)
    for s, rows in ((0, p_in.at[0]), (1, p_p.at[1, pl.ds(1, 3)])):
        for copy, cond in parent_copies(s, rows):
            pl.when(cond)(copy.wait_send)
    pl.when(~last)(parent_u_copy().wait_send)
    for wait in finish:
        wait()
    take_feedback(1, p_out.at[0])
    for copy in outs:
        copy.wait()


def put_out(p, u, v, p_out, u_out, v_out, sem):
    copies = [pltpu.make_async_copy(a, b, sem.at[i]) for i, (a, b) in enumerate(((p, p_out), (u, u_out), (v, v_out)))]
    for copy in copies:
        copy.start()
    for copy in copies:
        copy.wait()


def per_device(n, tiles, pressure, u_wind, v_wind, stiffness, vertical, nest_row0, nest_col0):
    fields = [jnp.transpose(x, (0, 2, 1, 3)) for x in (pressure, u_wind, v_wind, stiffness)]
    operands = [pltpu.with_memory_space_constraint(x, pltpu.HBM) for x in (nest_row0, nest_col0, vertical, *fields)]
    _, rows, levels, cols = fields[0].shape
    win = cols // RATIO
    row = (levels, cols)
    vmem = lambda *shape: pltpu.VMEM(shape, F32)
    dma = lambda *shape: pltpu.SemaphoreType.DMA(shape)

    owners = lambda rows, at: (at + rows - 1) // RATIO - at // RATIO + 1

    def most(rows):
        return max(owners(rows, at) for at in range(RATIO))

    def call(lead):
        return pl.pallas_call(
            functools.partial(kernel, n, tiles, lead),
            out_shape=[pltpu.VMEM((2, rows) + row, F32)] * 3,
            in_specs=[pl.BlockSpec(memory_space=pl.ANY)] * 7,
            out_specs=[pl.BlockSpec(memory_space=pltpu.VMEM)] * 3,
            scratch_shapes=[
                vmem(7, 7, *row), vmem(6, *row), vmem(5, *row), vmem(5, *row),
                vmem(3, 5, *row), vmem(4, *row), vmem(3, *row), vmem(3, *row),
                vmem(OUTER, 8, 128), vmem(OUTER, most(GROUP + 2), 8, 128), vmem(OUTER, levels, win), vmem(OUTER, most(GROUP), levels, win),
                vmem(OUTER, levels, win), vmem(OUTER, most(GROUP), levels, win), vmem(OUTER, *row), vmem(OUTER, *row),
                vmem(OUTER, 3, 2, levels, 128), vmem(OUTER, levels, win), vmem(OUTER, GROUP + 2, levels, win),
                pltpu.VMEM((cols, win), BF16), pltpu.VMEM((levels, 3 * levels), BF16),
                pltpu.SMEM(nest_row0.shape, jnp.int32), pltpu.SMEM(nest_col0.shape, jnp.int32), vmem(*vertical.shape),
                dma(11), dma(5), dma(2, 3), dma(2, 3), dma(3, 2, 2), dma(3, 2, 2), dma(2, 2), dma(2, 2), dma(2, 3), dma(2, 3),
                dma(OUTER, GROUP + 4), dma(OUTER, most(GROUP + 2)), dma(OUTER, 2), dma(OUTER, most(GROUP)), dma(OUTER, most(GROUP)),
                dma(OUTER, most(GROUP)), dma(OUTER, GROUP + 2),
            ],
            compiler_params=pltpu.CompilerParams(
                collective_id=lead // GROUP, has_side_effects=True, vmem_limit_bytes=48 * 1024 * 1024
            ),
            cost_estimate=pl.CostEstimate(flops=300_000_000, bytes_accessed=4_200_000, transcendentals=0),
        )
    branches = [lambda *args, lead=lead: tuple(call(lead)(*args)) for lead in range(1, LAST_X0 + 1, GROUP)]
    outs = lax.switch((nest_row0[0] - 1) // GROUP, branches, *operands)
    outs = pl.pallas_call(
        put_out,
        out_shape=[jax.ShapeDtypeStruct((2, rows) + row, F32)] * 3,
        in_specs=[pl.BlockSpec(memory_space=pltpu.VMEM)] * 3,
        out_specs=[pl.BlockSpec(memory_space=pl.ANY)] * 3,
        scratch_shapes=[dma(3)],
    )(*[pltpu.with_memory_space_constraint(x, pltpu.VMEM) for x in outs])
    return tuple(jnp.transpose(x, (0, 2, 1, 3)) for x in outs)


def solution(mesh):
    spec = P(None, None, ("grp", "tile"), None)
    tiles = mesh.shape["tile"]
    return jax.shard_map(
        functools.partial(per_device, mesh.shape["grp"] * tiles, tiles),
        mesh=mesh,
        in_specs=(spec, spec, spec, spec, P(), P(), P()),
        out_specs=(spec, spec, spec),
        check_vma=False,
    )
```

```python
import functools

import jax
import jax.numpy as jnp
from jax import lax
from jax.experimental import pallas as pl
from jax.experimental.pallas import tpu as pltpu
from jax.sharding import PartitionSpec as P

RATIO = 3
OUTER = 2
BLOCKS = 3
COURANT = 0.3
MIXING = 0.15
LAST_X0 = 60
GROUP = 6
MESH = pl.DeviceIdType.MESH
F32 = jnp.float32
EARLY = 1
BF16 = jnp.bfloat16


def pieces(x):
    a = x.astype(BF16)
    rest = x - a.astype(F32)
    b = rest.astype(BF16)
    c = (rest - b.astype(F32)).astype(BF16)
    return a, b, c


def kernel(
    n, tiles, lead,
    row0_in, col0_in, vert_in, p_in, u_in, v_in, k_in,
    p_out, u_out, v_out,
    n_p, n_u, n_v, n_k, p_p, p_u, p_v, p_k,
    g_send, g_recv, a_send, a_recv, b_send, b_recv, a_row, b_row, edge, f_send, f_recv, fold, mix,
    row0_ref, col0_ref, vert_ref,
    in_sem, out_sem, ni_send, ni_recv, nx_send, nx_recv, nm_send, nm_recv, px_send, px_recv,
    gs_send, gs_recv, e_send, a_sems, b_sems, f_sends, f_recvs,
):
    levels, cols = n_k.shape[1], n_k.shape[2]
    win = cols // RATIO
    me = lax.axis_index("grp") * tiles + lax.axis_index("tile")
    first, last = me == 0, me == n - 1
    own = RATIO * me

    def dev(d):
        d = d + 0 * me
        return (d // tiles, d % tiles)

    def remote(src, dst, s_sem, r_sem, to):
        return pltpu.make_async_remote_copy(
            src_ref=src, dst_ref=dst, send_sem=s_sem, recv_sem=r_sem, device_id=dev(to), device_id_type=MESH
        )

    def loop(low, high, body):
        lax.fori_loop(low, high, lambda i, _: (body(i), 0)[1], 0)

    def rows_of(count, body):
        for i in range(count):
            body(i)

    def arrived(ref, sem, cond=True):
        @pl.when(cond)
        def _():
            pltpu.make_async_copy(ref, ref, sem).wait()

    small = [
        pltpu.make_async_copy(src, dst, in_sem.at[8 + i])
        for i, (src, dst) in enumerate(((row0_in, row0_ref), (col0_in, col0_ref), (vert_in, vert_ref)))
    ]
    for copy in small:
        copy.start()
    loads = {}
    for at, (name, src, g, dst) in enumerate((
        ("pp", p_in, 0, p_p.at[0, pl.ds(1, 3)]), ("pv", v_in, 0, p_v), ("pu", u_in, 0, p_u.at[pl.ds(1, 3)]),
        ("np", p_in, 1, n_p.at[0, pl.ds(2, 3)]), ("nu", u_in, 1, n_u.at[pl.ds(2, 3)]),
        ("nv", v_in, 1, n_v.at[pl.ds(1, 3)]), ("nk", k_in, 1, n_k.at[pl.ds(1, 3)]), ("pk", k_in, 0, p_k),
    )):
        loads[name] = pltpu.make_async_copy(src.at[g], dst, in_sem.at[at])
        loads[name].start()

    ghosts_from, ghosts_to = g_recv.shape[1], GROUP + 4
    backs_to, backs_from = f_sends.shape[1], f_recv.shape[1]

    def ghost_to(k):
        d = own - lead + k - GROUP
        return d, (d >= 0) & (d < n), me - (d + lead + 2) // RATIO + 1

    def ghost_from(i):
        e = (me + lead + 2) // RATIO - 1 + i
        return e, (e >= 0) & (RATIO * e <= lead + me + GROUP)

    def back_to(i):
        e = (me + lead) // RATIO + i
        return e, RATIO * e < lead + me + GROUP, jnp.clip(me + lead - RATIO * e + GROUP - 1, 0, backs_from - 1)

    def back_from(k):
        d = own - lead + k - GROUP + 1
        return d, (d >= 0) & (d < n)

    a_from = tuple(range((lead + n) // RATIO, (lead + n + GROUP - 1) // RATIO + 1))
    b_from = tuple(range((lead - 1) // RATIO, (lead + GROUP - 2) // RATIO + 1))

    bar = pltpu.get_barrier_semaphore()
    count = jnp.where(first | last, 1, 2)

    def hello(d, cond):
        @pl.when(cond)
        def _():
            pl.semaphore_signal(bar, inc=1, device_id=dev(d), device_id_type=MESH)
    hello(me + 1, ~last)
    hello(me - 1, ~first)
    for i in range(ghosts_from):
        e, cond = ghost_from(i)
        hello(e, cond & (e != me))
    for k in range(ghosts_to):
        d, cond, _ = ghost_to(k)
        count = count + jnp.where(cond & (d != me), 1, 0)
    for k in range(backs_from):
        d, cond = back_from(k)
        hello(d, cond & (d != me))
    for i in range(backs_to):
        e, cond, _ = back_to(i)
        count = count + jnp.where(cond & (e != me), 1, 0)
    for e in a_from:
        hello(e, last)
        count = count + jnp.where(me == e, 1, 0)
    for e in b_from:
        if e > 0:
            hello(e, first)
            count = count + jnp.where(me == e, 1, 0)
    pl.semaphore_wait(bar, count)

    def parent_u_copy():
        return remote(u_in.at[0, 2], p_u.at[0], px_send.at[0, 2], px_recv.at[0, 2], me + 1)

    def parent_copies(s, rows):
        return (
            (remote(rows.at[2], p_p.at[s, 0], px_send.at[s, 0], px_recv.at[s, 0], me + 1), ~last),
            (remote(rows.at[0], p_p.at[s, 4], px_send.at[s, 1], px_recv.at[s, 1], me - 1), ~first),
        )

    to_up = (
        (p_in.at[1, 2], n_p.at[0, 1], nx_send.at[0, 0, 1], nx_recv.at[0, 0, 1]),
        (p_in.at[1, 1], n_p.at[0, 0], nx_send.at[0, 0, 0], nx_recv.at[0, 0, 0]),
        (u_in.at[1, pl.ds(1, 2)], n_u.at[pl.ds(0, 2)], ni_send.at[0, 0], ni_recv.at[0, 0]),
        (v_in.at[1, 2], n_v.at[0], ni_send.at[0, 1], ni_recv.at[0, 1]),
        (k_in.at[1, 2], n_k.at[0], ni_send.at[0, 2], ni_recv.at[0, 2]),
    )
    to_down = (
        (p_in.at[1, 0], n_p.at[0, 5], nx_send.at[0, 1, 0], nx_recv.at[0, 1, 0]),
        (p_in.at[1, 1], n_p.at[0, 6], nx_send.at[0, 1, 1], nx_recv.at[0, 1, 1]),
        (u_in.at[1, 0], n_u.at[5], ni_send.at[1, 0], ni_recv.at[1, 0]),
        (v_in.at[1, 0], n_v.at[4], ni_send.at[1, 1], ni_recv.at[1, 1]),
        (k_in.at[1, 0], n_k.at[4], ni_send.at[1, 2], ni_recv.at[1, 2]),
    )
    def first_copies(low, high):
        for i in range(low, high):
            for group, to, cond in ((to_up, me + 1, ~last), (to_down, me - 1, ~first)):
                yield remote(*group[i], to), cond

    for copy, cond in first_copies(0, EARLY):
        pl.when(cond)(copy.start)

    for copy in small:
        copy.wait()
    x0, y0 = row0_ref[0], col0_ref[0]
    rest = x0 - lead
    lane = lax.broadcasted_iota(jnp.int32, (levels, cols), 1)
    lane128 = lax.broadcasted_iota(jnp.int32, (levels, 128), 1)
    level128 = lax.broadcasted_iota(jnp.int32, (levels, 128), 0)
    row8 = lax.broadcasted_iota(jnp.int32, (8, 128), 0)

    def ghost_copy(o, k):
        d, cond, slot = ghost_to(k)
        return remote(g_send.at[o], g_recv.at[o, slot], gs_send.at[o, k], gs_recv.at[o, slot], d), cond & (d != me)

    def row_copies(o):
        for i, e in enumerate(a_from):
            yield remote(a_send.at[o], a_recv.at[o, i], e_send.at[o, 0], a_sems.at[o, i], n - 1), me == e
        for i, e in enumerate(b_from):
            if e > 0:
                yield remote(b_send.at[o], b_recv.at[o, i], e_send.at[o, 1], b_sems.at[o, i], 0), me == e

    def start_ghosts(o):
        pp, pu = p_p.at[o, pl.ds(1, 3)], p_u.at[pl.ds(1, 3)]

        def gather(j, total):
            right = jnp.sum(jnp.where(lane == y0 + win, pp[j], 0.0), axis=1, keepdims=True)
            left = jnp.sum(jnp.where(lane == y0 - 1, p_v[j], 0.0), axis=1, keepdims=True)
            both = jnp.where(level128 == lane128, right, 0.0) + jnp.where(level128 == lane128 - levels, left, 0.0)
            return jnp.where(row8 == j, jnp.sum(both, axis=0, keepdims=True), total)
        g_send[o] = lax.fori_loop(0, RATIO, gather, jnp.zeros((8, 128), F32))

        def column(k):
            d, cond, slot = ghost_to(k)

            @pl.when(cond & (d == me))
            def _():
                g_recv[o, slot] = g_send[o]
            copy, cond = ghost_copy(o, k)
            pl.when(cond)(copy.start)
        loop(0, ghosts_to, column)

        def pick_row(field, target):
            out = jnp.zeros((levels, cols), F32)
            for j in range(RATIO):
                out = jnp.where(target == own + j, field[j], out)
            return pltpu.roll(out, cols - y0, axis=1)[:, :win]

        @pl.when((me >= a_from[0]) & (me <= a_from[-1]))
        def _():
            a_send[o] = pick_row(pp, x0 + n)

        @pl.when((me >= b_from[0]) & (me <= b_from[-1]))
        def _():
            b_send[o] = pick_row(pu, x0 - 1)
        if b_from[0] == 0:
            @pl.when(first)
            def _():
                b_recv[o, 0] = b_send[o]
        for copy, cond in row_copies(o):
            pl.when(cond)(copy.start)

    def end_ghosts(o):
        def column(k):
            copy, cond = ghost_copy(o, k)
            pl.when(cond)(copy.wait_send)
        loop(0, ghosts_to, column)
        for copy, cond in row_copies(o):
            pl.when(cond)(copy.wait_send)

    def take_ghosts(o):
        for i in range(ghosts_from):
            e, cond = ghost_from(i)
            arrived(g_recv.at[o, i], gs_recv.at[o, i], cond & (e != me))
        for t in range(3):
            place = (me + lead + 2) % RATIO + rest + t
            row = jnp.zeros((1, 128), F32)
            for i in range(ghosts_from):
                row = row + jnp.sum(jnp.where(row8 == place - RATIO * i, g_recv[o, i], 0.0), axis=0, keepdims=True)
            right = jnp.sum(jnp.where(level128 == lane128, row, 0.0), axis=1, keepdims=True)
            left = jnp.sum(jnp.where(level128 == lane128 - levels, row, 0.0), axis=1, keepdims=True)
            edge[o, t, 0] = jnp.broadcast_to(right, (levels, 128))
            edge[o, t, 1] = jnp.broadcast_to(left, (levels, 128))

        @pl.when(first | last)
        def _():
            a = b = jnp.zeros((levels, win), F32)
            for i, e in enumerate(a_from):
                arrived(a_recv.at[o, i], a_sems.at[o, i], last)
                a = jnp.where((x0 + n >= RATIO * e) & (x0 + n < RATIO * (e + 1)), a_recv[o, i], a)
            for i, e in enumerate(b_from):
                if e > 0:
                    arrived(b_recv.at[o, i], b_sems.at[o, i], first)
                b = jnp.where((x0 - 1 >= RATIO * e) & (x0 - 1 < RATIO * (e + 1)), b_recv[o, i], b)
            x = jnp.where(jnp.broadcast_to(last.astype(jnp.int32), a.shape) > 0, a, b)
            wide = lax.dot_general(
                jnp.concatenate(pieces(x), axis=0), fold[...], (((1,), (1,)), ((), ())), preferred_element_type=F32
            )
            wide = (wide[:levels] + wide[levels:2 * levels]) + wide[2 * levels:]
            a_row[o] = wide
            b_row[o] = wide

    def from_right(x, ghost):
        moved = pltpu.roll(x, cols - 1, axis=1)
        if ghost is None:
            return moved
        tail = jnp.where(lane128 == 127, ghost, moved[:, cols - 128:])
        return jnp.concatenate([moved[:, :cols - 128], tail], axis=1)

    def from_left(x, ghost):
        moved = pltpu.roll(x, 1, axis=1)
        if ghost is None:
            return moved
        head = jnp.where(lane128 == 0, ghost, moved[:, :128])
        return jnp.concatenate([head, moved[:, 128:]], axis=1)

    def new_pressure(p, k, u, below, v, left):
        q = p - k * ((u - below) + (v - from_left(v, left)))
        a = q.astype(BF16)
        b = (q - a.astype(F32)).astype(BF16)
        return q + jnp.dot(mix[...], jnp.concatenate([a, b, a], axis=0), preferred_element_type=F32)

    def nest_u(s, i):
        n_u[i] = n_u[i] - COURANT * (n_p[s, i + 1] - n_p[s, i])

    def nest_v(s, o, i, t):
        p = n_p[s, i + 1]
        v = n_v[i] - COURANT * (from_right(p, edge[o, t, 0]) - p)
        n_v[i] = v
        return p, v

    def below_nest(o):
        @pl.when(first)
        def _():
            n_u[1] = b_row[o]

    def above_nest(s, o):
        @pl.when(last)
        def _():
            n_p[s, 5] = a_row[o]

    def nest_row(s, o, i, t):
        p, v = nest_v(s, o, i, t)
        n_p[s + 1, i + 1] = new_pressure(p, n_k[i], n_u[i + 1], n_u[i], v, edge[o, t, 1])

    def middle_copies(blk):
        s = 2 * blk + 1
        return (
            (remote(n_p.at[s, 3], n_p.at[s, 0], nm_send.at[blk, 0], nm_recv.at[blk, 0], me + 1), ~last),
            (remote(n_p.at[s, 3], n_p.at[s, 6], nm_send.at[blk, 1], nm_recv.at[blk, 1], me - 1), ~first),
        )

    def end_copies(blk):
        s, nxt = 2 * blk + 2, blk + 1
        up = [remote(n_p.at[s, i + 3], n_p.at[s, i], nx_send.at[nxt, 0, i], nx_recv.at[nxt, 0, i], me + 1) for i in range(2)]
        down = [remote(n_p.at[s, i + 2], n_p.at[s, i + 5], nx_send.at[nxt, 1, i], nx_recv.at[nxt, 1, i], me - 1) for i in range(2)]
        return up, down

    def nest_block(blk):
        s = 2 * blk
        before, after = blk // 2, (blk + 1) // 2
        more = blk < BLOCKS - 1
        up, down = end_copies(blk)

        pl.when(blk == 0)(lambda: take_ghosts(0))
        for i in (2, 3):
            nest_u(s, i)
        nest_row(s, before, 2, 1)

        @pl.when(more)
        def _():
            for copy, cond in middle_copies(blk):
                pl.when(cond)(copy.start)

        @pl.when(blk > 0)
        def _():
            arrived(n_p.at[s - 1, 0], nm_recv.at[blk - 1, 0], ~first)
            arrived(n_p.at[s - 1, 6], nm_recv.at[blk - 1, 1], ~last)
            nest_u(s - 1, 0)
            nest_u(s - 1, 5)
            nest_v(s - 1, before, 0, 0)
            nest_v(s - 1, before, 4, 2)
        for i in range(2):
            arrived(n_p.at[s, i], nx_recv.at[blk, 0, i], ~first)
            arrived(n_p.at[s, 5 + i], nx_recv.at[blk, 1, i], ~last)

        @pl.when(blk == 0)
        def _():
            arrived(to_up[2][1], ni_recv.at[0, 0], ~first)
            arrived(to_down[2][1], ni_recv.at[1, 0], ~last)
        above_nest(s, before)
        for i in (0, 1, 4, 5):
            nest_u(s, i)
        below_nest(before)
        nest_row(s, before, 3, 1)
        nest_row(s, before, 1, 1)
        pl.when(blk == 1)(lambda: take_ghosts(1))

        for i in (2, 3):
            nest_u(s + 1, i)
        nest_row(s + 1, after, 2, 1)
        pl.when(more & ~last)(up[0].start)
        pl.when(more & ~first)(down[1].start)

        @pl.when(blk == 0)
        def _():
            for i in (1, 2):
                arrived(to_up[i + 2][1], ni_recv.at[0, i], ~first)
                arrived(to_down[i + 2][1], ni_recv.at[1, i], ~last)
            for i in (0, 4):
                n_k[i] = COURANT * n_k[i]
        nest_row(s, before, 4, 2)
        above_nest(s + 1, after)
        nest_u(s + 1, 4)
        nest_row(s + 1, after, 3, 1)
        pl.when(more & ~last)(up[1].start)
        nest_row(s, before, 0, 0)
        nest_u(s + 1, 1)
        below_nest(after)
        nest_row(s + 1, after, 1, 1)
        pl.when(more & ~first)(down[0].start)

    def parent_substep(s):
        arrived(p_p.at[s, 0], px_recv.at[s, 0], ~first)
        arrived(p_p.at[s, 4], px_recv.at[s, 1], ~last)
        for i in range(4):
            p_u[i] = p_u[i] - COURANT * (p_p[s, i + 1] - p_p[s, i])

        @pl.when(first)
        def _():
            p_u[0] = jnp.zeros((levels, cols), F32)

        @pl.when(last)
        def _():
            p_u[3] = jnp.zeros((levels, cols), F32)

        def row(r):
            p = p_p[s, r + 1]
            v = p_v[r] - COURANT * (from_right(p, None) - p)
            p_v[r] = v
            p_p[s + 1, r + 1] = new_pressure(p, p_k[r], p_u[r + 1], p_u[r], v, None)
        rows_of(RATIO, row)

    def back_copy(o, i):
        e, cond, slot = back_to(i)
        return remote(f_send.at[o], f_recv.at[o, slot], f_sends.at[o, i], f_recvs.at[o, slot], e), cond & (e != me)

    def start_feedback(o):
        rows = n_p.at[3 * (o + 1)]
        stack = jnp.concatenate(pieces((rows[2] + rows[3]) + rows[4]), axis=0)
        mean = jnp.dot(stack, fold[...], preferred_element_type=F32)
        f_send[o] = ((mean[:levels] + mean[levels:2 * levels]) + mean[2 * levels:]) * (1.0 / (RATIO * RATIO))
        for i in range(backs_to):
            e, cond, slot = back_to(i)

            @pl.when(cond & (e == me))
            def _():
                f_recv[o, slot] = f_send[o]
            copy, cond = back_copy(o, i)
            pl.when(cond)(copy.start)

    def take_feedback(o, target):
        for k in range(backs_from):
            d, cond = back_from(k)
            arrived(f_recv.at[o, k], f_recvs.at[o, k], cond & (d != me))
        under = (lane >= y0) & (lane < y0 + win)

        def place(j):
            row = own + j
            value = f_recv[o, j + GROUP - 1]
            for i in range(1, GROUP):
                value = jnp.where(rest == i, f_recv[o, j + GROUP - 1 - i], value)
            value = pltpu.roll(jnp.concatenate([value, jnp.zeros((levels, cols - win), F32)], axis=1), y0, axis=1)
            inside = ((row >= x0) & (row < x0 + n)).astype(jnp.int32)
            target[j] = jnp.where(under & (jnp.broadcast_to(inside, (levels, cols)) > 0), value, p_p[o + 1, j + 1])
        loop(0, RATIO, place)

    for name in ("pp", "pv", "pu"):
        loads[name].wait()
    spot = lax.broadcasted_iota(jnp.int32, (cols, win), 0) - RATIO * lax.broadcasted_iota(jnp.int32, (cols, win), 1)

    def stores():
        pairs = (
            (n_p.at[6, pl.ds(2, 3)], p_out.at[1]), (n_u.at[pl.ds(2, 3)], u_out.at[1]), (n_v.at[pl.ds(1, 3)], v_out.at[1]),
            (p_u.at[pl.ds(1, 3)], u_out.at[0]), (p_v, v_out.at[0]),
        )
        return [pltpu.make_async_copy(src, dst, out_sem.at[i]) for i, (src, dst) in enumerate(pairs)]

    def turn(it):
        pl.when(it < OUTER)(lambda: start_ghosts(it))

        @pl.when(it == 0)
        def _():
            for copy, cond in first_copies(EARLY, 5):
                pl.when(cond)(copy.start)
            for copy, cond in parent_copies(0, p_in.at[0]):
                pl.when(cond)(copy.start)
            pl.when(~last)(parent_u_copy().start)

        @pl.when(it == 0)
        def _():
            fold[...] = jnp.where((spot >= 0) & (spot < RATIO), 1.0, 0.0).astype(BF16)
            block = lax.broadcasted_iota(jnp.int32, (levels, 3 * levels), 1)
            copies = (block % levels == lax.broadcasted_iota(jnp.int32, (levels, 3 * levels), 0)).astype(F32)
            wide = jnp.dot(MIXING * vert_ref[...], copies, precision=lax.Precision.HIGHEST, preferred_element_type=F32)
            m1, m2, _ = (x.astype(F32) for x in pieces(wide))
            mix[...] = jnp.where(block >= 2 * levels, m2, m1).astype(BF16)
            for name in ("np", "nu", "nv", "nk", "pk"):
                loads[name].wait()
            for i in range(RATIO):
                p_k[i] = COURANT * p_k[i]
                n_k[i + 1] = COURANT * n_k[i + 1]
        nest_block(it)

        @pl.when(it == 2)
        def _():
            take_feedback(0, p_p.at[1, pl.ds(1, 3)])
            for copy, cond in parent_copies(1, p_p.at[1, pl.ds(1, 3)]):
                pl.when(cond)(copy.start)
        pl.when(it > 0)(lambda: start_feedback(it - 1))

        @pl.when(it == 2)
        def _():
            for copy in stores()[:3]:
                copy.start()
        pl.when(it == 0)(lambda: arrived(p_u.at[0], px_recv.at[0, 2], ~first))
        pl.when(it != 1)(lambda: parent_substep(it // 2))
    loop(0, BLOCKS, turn)
    outs = stores()
    for copy in outs[3:]:
        copy.start()
    for o in range(OUTER):
        end_ghosts(o)
        for i in range(backs_to):
            copy, cond = back_copy(o, i)
            pl.when(cond)(copy.wait_send)
    for blk in range(BLOCKS - 1):
        for copy, cond in middle_copies(blk):
            pl.when(cond)(copy.wait_send)
        up, down = end_copies(blk)
        for i in range(2):
            pl.when(~last)(up[i].wait_send)
            pl.when(~first)(down[i].wait_send)
    for s, rows in ((0, p_in.at[0]), (1, p_p.at[1, pl.ds(1, 3)])):
        for copy, cond in parent_copies(s, rows):
            pl.when(cond)(copy.wait_send)
    pl.when(~last)(parent_u_copy().wait_send)
    for copy, cond in first_copies(0, 5):
        pl.when(cond)(copy.wait_send)
    take_feedback(1, p_out.at[0])
    for copy in outs:
        copy.wait()


def put_out(p, u, v, p_out, u_out, v_out, sem):
    copies = [pltpu.make_async_copy(a, b, sem.at[i]) for i, (a, b) in enumerate(((p, p_out), (u, u_out), (v, v_out)))]
    for copy in copies:
        copy.start()
    for copy in copies:
        copy.wait()


def per_device(n, tiles, pressure, u_wind, v_wind, stiffness, vertical, nest_row0, nest_col0):
    fields = [jnp.transpose(x, (0, 2, 1, 3)) for x in (pressure, u_wind, v_wind, stiffness)]
    operands = [pltpu.with_memory_space_constraint(x, pltpu.HBM) for x in (nest_row0, nest_col0, vertical, *fields)]
    _, rows, levels, cols = fields[0].shape
    win = cols // RATIO
    row = (levels, cols)
    vmem = lambda *shape: pltpu.VMEM(shape, F32)
    dma = lambda *shape: pltpu.SemaphoreType.DMA(shape)

    owners = lambda rows, at: (at + rows - 1) // RATIO - at // RATIO + 1

    def most(rows):
        return max(owners(rows, at) for at in range(RATIO))

    def call(lead):
        return pl.pallas_call(
            functools.partial(kernel, n, tiles, lead),
            out_shape=[pltpu.VMEM((2, rows) + row, F32)] * 3,
            in_specs=[pl.BlockSpec(memory_space=pl.ANY)] * 7,
            out_specs=[pl.BlockSpec(memory_space=pltpu.VMEM)] * 3,
            scratch_shapes=[
                vmem(7, 7, *row), vmem(6, *row), vmem(5, *row), vmem(5, *row),
                vmem(3, 5, *row), vmem(4, *row), vmem(3, *row), vmem(3, *row),
                vmem(OUTER, 8, 128), vmem(OUTER, most(GROUP + 2), 8, 128), vmem(OUTER, levels, win), vmem(OUTER, most(GROUP), levels, win),
                vmem(OUTER, levels, win), vmem(OUTER, most(GROUP), levels, win), vmem(OUTER, *row), vmem(OUTER, *row),
                vmem(OUTER, 3, 2, levels, 128), vmem(OUTER, levels, win), vmem(OUTER, GROUP + 2, levels, win),
                pltpu.VMEM((cols, win), BF16), pltpu.VMEM((levels, 3 * levels), BF16),
                pltpu.SMEM(nest_row0.shape, jnp.int32), pltpu.SMEM(nest_col0.shape, jnp.int32), vmem(*vertical.shape),
                dma(11), dma(5), dma(2, 3), dma(2, 3), dma(3, 2, 2), dma(3, 2, 2), dma(2, 2), dma(2, 2), dma(2, 3), dma(2, 3),
                dma(OUTER, GROUP + 4), dma(OUTER, most(GROUP + 2)), dma(OUTER, 2), dma(OUTER, most(GROUP)), dma(OUTER, most(GROUP)),
                dma(OUTER, most(GROUP)), dma(OUTER, GROUP + 2),
            ],
            compiler_params=pltpu.CompilerParams(
                collective_id=lead // GROUP, has_side_effects=True, vmem_limit_bytes=48 * 1024 * 1024
            ),
            cost_estimate=pl.CostEstimate(flops=300_000_000, bytes_accessed=4_200_000, transcendentals=0),
        )
    branches = [lambda *args, lead=lead: tuple(call(lead)(*args)) for lead in range(1, LAST_X0 + 1, GROUP)]
    outs = lax.switch((nest_row0[0] - 1) // GROUP, branches, *operands)
    outs = pl.pallas_call(
        put_out,
        out_shape=[jax.ShapeDtypeStruct((2, rows) + row, F32)] * 3,
        in_specs=[pl.BlockSpec(memory_space=pltpu.VMEM)] * 3,
        out_specs=[pl.BlockSpec(memory_space=pl.ANY)] * 3,
        scratch_shapes=[dma(3)],
    )(*[pltpu.with_memory_space_constraint(x, pltpu.VMEM) for x in outs])
    return tuple(jnp.transpose(x, (0, 2, 1, 3)) for x in outs)


def solution(mesh):
    spec = P(None, None, ("grp", "tile"), None)
    tiles = mesh.shape["tile"]
    return jax.shard_map(
        functools.partial(per_device, mesh.shape["grp"] * tiles, tiles),
        mesh=mesh,
        in_specs=(spec, spec, spec, spec, P(), P(), P()),
        out_specs=(spec, spec, spec),
        check_vma=False,
    )
```
